32 devices in a mesh: section: 2 (over y), mp: 4 (over x, core), dp: 4 (over z).
Axes of the slice: x: 2, y: 2, z: 4, core: 2. Of those that a mesh axis runs over, the one named last changes fastest.
Arguments:
- saved_inputs: bfloat16 [2, 8, 512, 8192], P('section', None, 'dp', 'mp'), may hold values from -40 to 40
- cotangent: bfloat16 [8, 512, 8192], P(None, 'dp', 'mp'), may hold values from -6 to 6
- weight_in: bfloat16 [2, 8192, 512], P('section', 'mp', 'dp'), may hold values from -0.0625 to 0.0625
- weight_out: bfloat16 [2, 8192, 512], P('section', 'mp', 'dp'), may hold values from -0.25 to 0.25
- gain: float32 [2, 8192], P(None, 'mp'), may hold values from 0.1 to 1.9
- plan: int32 [8], replicated, may hold values from 0 to 7, each once
Outputs:
- grad_in: float32 [2, 8192, 512], P('section', 'mp', 'dp')
- grad_out: float32 [2, 8192, 512], P('section', 'mp', 'dp')
- input_grads: bfloat16 [2, 8, 512, 8192], P('section', None, 'dp', 'mp')
The draws below stay inside these ranges and needn't reach their ends.
All inputs are finite; a program needn't handle non-finite values.
Results may differ from the reference program's by a relative error of at most 0.02.
Values may be sent and summed in bfloat16 or wider, within the bound.
No kernel may reach another device: no remote copies, remote signals or barrier semaphores. Data moves between devices by JAX's collectives and lax.ppermute only.
A program may use at most 128 MiB of HBM per device.

```python
import jax
import jax.numpy as jnp
from jax import lax

D = 8192
E = 512
SLOTS = 8
TOKENS = 512
N_SECTION = 2
N_MP = 4


def draw_saved_inputs(key, part):
    key = jax.random.fold_in(key, 11)
    base_key, row_key = jax.random.split(key, 2)
    full_shape = (N_SECTION, SLOTS, TOKENS, D)
    columns = jnp.exp(jnp.log(10.0) * (jnp.arange(D, dtype=jnp.float32) / D - 0.5))
    base_draw = jnp.clip(jax.random.normal(base_key, full_shape, jnp.float32), -4.0, 4.0)
    row_scale = jnp.exp(jax.random.uniform(row_key, (N_SECTION, SLOTS, TOKENS, 1), jnp.float32, jnp.log(0.3162), jnp.log(3.162)))
    return (base_draw * row_scale * columns).astype(jnp.bfloat16)


def block_levels(key, shape, cuts, low, high):
    def one(dim, blocks):
        heights = jax.random.uniform(jax.random.fold_in(jax.random.fold_in(key, 6), dim), (blocks,), jnp.float32, low / len(cuts), high / len(cuts))
        return jnp.repeat(jnp.exp(heights), shape[dim] // blocks).reshape((-1,) + (1,) * (len(shape) - dim - 1))

    level = one(*cuts[0])
    for cut in cuts[1:]:
        level = level * one(*cut)
    return level


def gaussian(stream_key, extent, deviation, most, shards=(), held_as=jnp.bfloat16):
    entries = jax.random.normal(stream_key, extent, jnp.float32) * deviation
    if len(shards) > 0:
        entries = block_levels(stream_key, extent, shards, -0.22, 0.18) * entries
    return jnp.clip(entries, min=-most, max=most).astype(held_as)


def setup_inputs(seed: int = 0) -> dict:
    arg_keys = jax.random.split(jax.random.key(seed), 7)
    return {
        "saved_inputs": draw_saved_inputs(jax.random.fold_in(arg_keys[6], 71), 0),
        "cotangent": gaussian(arg_keys[1], (SLOTS, TOKENS, D), 1.0, 6.0, ((1, 4), (2, 4))),
        "weight_in": gaussian(arg_keys[2], (N_SECTION, D, E), D ** -0.5, 0.0625, ((0, 2), (1, 4), (2, 4))),
        "weight_out": gaussian(arg_keys[3], (N_SECTION, D, E), E ** -0.5, 0.25, ((0, 2), (1, 4), (2, 4))),
        "gain": jnp.clip(1.0 + 0.18 * jax.random.normal(arg_keys[4], (N_SECTION, D), jnp.float32), 0.1, 1.9),
        "plan": jax.random.permutation(arg_keys[5], SLOTS).astype(jnp.int32),
    }


EPS = 1e-05

def block_back(stored, incoming, proj_in, proj_out, gain_row):
    stored_wide = stored.astype(jnp.float32)
    normed = (stored_wide * gain_row).astype(jnp.bfloat16)
    inverse_rms = lax.rsqrt(lax.optimization_barrier(jnp.mean(stored_wide * stored_wide, axis=-1, keepdims=True)) + EPS)
    unit_sums = jnp.dot(normed, proj_in, preferred_element_type=jnp.float32)
    hidden_pre = inverse_rms * unit_sums
    activated = jax.nn.silu(hidden_pre).astype(jnp.bfloat16)
    token_count = incoming.shape[0]
    grad_blocks = incoming.astype(jnp.float32).reshape(token_count, N_MP, D // N_MP)
    proj_blocks = proj_out.astype(jnp.float32).reshape(N_MP, D // N_MP, E)
    pieces = jnp.einsum('tjd,jde->jte', grad_blocks, proj_blocks)
    pieces = lax.optimization_barrier(pieces.astype(jnp.bfloat16))
    unit_grads = lax.optimization_barrier(jnp.sum(pieces.astype(jnp.float32), axis=0))
    sigma = jax.nn.sigmoid(hidden_pre)
    grad_hidden = unit_grads * sigma * (1.0 + hidden_pre * (1.0 - sigma))
    scaled_grad = (inverse_rms * grad_hidden).astype(jnp.bfloat16)
    back_proj = jnp.dot(scaled_grad, proj_in.T, preferred_element_type=jnp.float32)
    rms_term = lax.optimization_barrier(jnp.sum(grad_hidden * unit_sums, axis=-1, keepdims=True))
    result = incoming.astype(jnp.float32) + gain_row * back_proj - inverse_rms ** 3 / D * rms_term * stored_wide
    grad_proj_in = jnp.dot(normed.T, scaled_grad, preferred_element_type=jnp.float32)
    grad_proj_out = jnp.dot(incoming.T, activated, preferred_element_type=jnp.float32)
    return (result.astype(jnp.bfloat16), grad_proj_in, grad_proj_out)

def reference(saved_inputs, cotangent, weight_in, weight_out, gain, plan):
    half_slots = SLOTS // 2
    totals_in = [jnp.zeros((D, E), jnp.float32) for group in range(N_SECTION)]
    totals_out = [jnp.zeros((D, E), jnp.float32) for group in range(N_SECTION)]
    results = [[None] * SLOTS for section in range(N_SECTION)]
    for slot in range(SLOTS):
        micro = plan[slot].astype(jnp.int32)
        incoming = lax.dynamic_index_in_dim(cotangent, micro, 0, keepdims=False)
        if slot < half_slots:
            section_order = list(range(N_SECTION - 1, -1, -1))
        else:
            section_order = list(range(N_SECTION))
        for section in section_order:
            group = section if slot < half_slots else N_SECTION - 1 - section
            incoming, part_in, part_out = block_back(saved_inputs[section, slot], incoming, weight_in[group], weight_out[group], gain[group])
            results[section][slot] = incoming
            totals_in[group] = totals_in[group] + part_in
            totals_out[group] = totals_out[group] + part_out
    input_grads = jnp.stack([jnp.stack(section_rows) for section_rows in results])
    return (jnp.stack(totals_in), jnp.stack(totals_out), input_grads)
```

```python
import jax
import jax.numpy as jnp
from jax import lax
from jax.sharding import PartitionSpec as P

EPS = 1e-05
F32 = jnp.float32
BF16 = jnp.bfloat16
PAD = 128


def rotate(block, shift):
    count = lax.axis_size("dp")
    return lax.ppermute(block, "dp", [(i, (i + shift) % count) for i in range(count)])


def gather_units(block):
    count = lax.axis_size("dp")
    return jnp.concatenate([block] + [rotate(block, -k) for k in range(1, count)], axis=-1)


def scatter_units(total):
    count = lax.axis_size("dp")
    width = total.shape[-1] // count
    parts = total.astype(BF16)
    kept = total[..., :width].astype(F32)
    for k in range(1, count):
        kept = kept + rotate(parts[..., k * width : (k + 1) * width], k).astype(F32)
    return kept


def swap_section(block):
    return lax.ppermute(block, "section", [(0, 1), (1, 0)])


def swap_core(block):
    return lax.ppermute(block, "mp", [(i, i ^ 1) for i in range(4)])


def swap_chip(block):
    return lax.ppermute(block, "mp", [(i, i ^ 2) for i in range(4)])


def swap_both(block):
    pairs = [(i, (i ^ 4) ^ 2) for i in range(8)]
    return lax.ppermute(block, ("section", "mp"), pairs)


def pick(array, index, axis):
    return lax.dynamic_index_in_dim(array, index, axis, keepdims=False)


def ordered(first, second, flipped, axis):
    return jnp.where(
        flipped,
        jnp.concatenate((second, first), axis),
        jnp.concatenate((first, second), axis),
    )


def pair_sum(partial):
    mp_index = lax.axis_index("mp")
    core, chip = mp_index % 2, mp_index // 2
    sets, slots, tokens, width = partial.shape
    parts = partial.reshape(sets, slots // 2, 2, tokens, width)
    narrow = parts.astype(BF16)
    mine = pick(parts, core, 2).astype(F32) + swap_core(pick(narrow, 1 - core, 2)).astype(F32)
    sent = mine.astype(BF16)
    total = pick(mine[0], chip, 0)
    total = total + swap_chip(pick(sent[0], 1 - chip, 0)).astype(F32)
    total = total + swap_section(pick(sent[1], chip, 0)).astype(F32)
    total = total + swap_both(pick(sent[1], 1 - chip, 0)).astype(F32)
    return total


def pair_spread(block):
    mp_index = lax.axis_index("mp")
    core, chip = mp_index % 2, mp_index // 2
    tokens, width = block.shape
    own = ordered(block[None], swap_chip(block)[None], chip == 1, 0)
    received = ordered(swap_section(block)[None], swap_both(block)[None], chip == 1, 0)
    mine = jnp.stack((own, received))
    both = ordered(mine[:, :, None], swap_core(mine)[:, :, None], core == 1, 2)
    return both.reshape(2, 4, tokens, width)


def any_sum(partial):
    sets, slots, tokens, width = partial.shape
    count = lax.axis_size("section") * lax.axis_size("mp")
    rows = partial.astype(BF16).reshape(count, sets * slots * tokens // count, width)
    moved = lax.all_to_all(rows, ("section", "mp"), 0, 0)
    return jnp.sum(moved.astype(F32), axis=0)


def any_spread(block, sets, slots, tokens):
    whole = lax.all_gather(block, ("section", "mp"), axis=0, tiled=True)
    return whole.reshape(sets, slots, tokens, block.shape[-1])


def row_terms(unit_sums, square_sums, features):
    inverse_rms = lax.rsqrt(square_sums / features + EPS)
    hidden_pre = inverse_rms * unit_sums
    sigma = jax.nn.sigmoid(hidden_pre)
    activated = (hidden_pre * sigma).astype(BF16)
    return inverse_rms, hidden_pre, sigma, activated


def unit_terms(unit_grads, unit_sums, inverse_rms, hidden_pre, sigma, features):
    grad_hidden = unit_grads * sigma * (1.0 + hidden_pre * (1.0 - sigma))
    scaled_grad = (inverse_rms * grad_hidden).astype(BF16)
    rms_term = jnp.sum(grad_hidden * unit_sums, axis=-1, keepdims=True)
    factor = inverse_rms**3 / features * rms_term
    return scaled_grad, factor


def project(rows, weights):
    return jnp.einsum("jktd,de->jkte", rows, weights, preferred_element_type=F32)


def accumulate(rows, units):
    return jnp.einsum("jktd,jkte->de", rows, units, preferred_element_type=F32)


def run_phase(stored, incoming, in_full, out_full, gain_row, features, sum_units, spread_units):
    units = in_full.shape[-1]
    wide = stored.astype(F32)
    normed = (wide * gain_row).astype(BF16)
    squares = jnp.sum(wide * wide, axis=-1, keepdims=True)
    part = project(normed, in_full)
    packed = jnp.concatenate((part, jnp.broadcast_to(squares, part.shape[:-1] + (PAD,))), axis=-1)
    hidden = sum_units(packed)
    unit_sums, square_sums = hidden[:, :units], hidden[:, units : units + 1]
    inverse_rms, hidden_pre, sigma, activated = row_terms(unit_sums, square_sums, features)
    activated = spread_units(activated)
    unit_grads = sum_units(project(incoming, out_full))
    scaled_grad, factor = unit_terms(
        unit_grads, unit_sums, inverse_rms, hidden_pre, sigma, features
    )
    factor = jnp.broadcast_to(factor.astype(BF16), (factor.shape[0], PAD))
    spread = spread_units(jnp.concatenate((scaled_grad, factor), axis=-1))
    scaled_grad, factor = spread[..., :units], spread[..., units : units + 1].astype(F32)
    back = jnp.einsum("jkte,de->jktd", scaled_grad, in_full, preferred_element_type=F32)
    result = (incoming.astype(F32) + gain_row * back - factor * wide).astype(BF16)
    return result, accumulate(normed, scaled_grad), accumulate(incoming, activated)


def two_sections(saved_inputs, cotangent, weight_in, weight_out, gain, plan):
    own = lax.axis_index("section")
    other = 1 - own
    stored = saved_inputs[0]
    slots, tokens, width = stored.shape
    half, part = slots // 2, width // 2
    features = width * lax.axis_size("mp")

    def columns(array, section):
        return lax.dynamic_slice_in_dim(array, section * part, part, array.ndim - 1)

    def rows(array, section):
        return lax.dynamic_slice_in_dim(array, section * part, part, 0)

    mine = jnp.stack((rows(weight_in[0], own), rows(weight_out[0], own)))
    moved = swap_section(jnp.stack((rows(weight_in[0], other), rows(weight_out[0], other))))
    sent_slots = [half * other, half * own]
    blocks = []
    for phase in range(2):
        local = lax.dynamic_slice_in_dim(stored, sent_slots[phase], half, 0)
        blocks.append((columns(local, own), swap_section(columns(local, other))))
    top = columns(cotangent, own)

    def chosen(start):
        return jnp.stack([pick(top, plan[start + i], 0) for i in range(half)])

    incoming = jnp.stack((chosen(sent_slots[0]), chosen(sent_slots[1])))
    outputs = jnp.zeros_like(stored)
    in_blocks = [None, None]
    out_blocks = [None, None]
    for phase in range(2):
        group = 1 - phase
        held = jnp.where(own == group, mine, moved)
        in_full = gather_units(held[0])
        out_full = gather_units(held[1])
        gain_row = columns(gain[group], own)
        result, in_total, out_total = run_phase(
            jnp.stack(blocks[phase]),
            incoming,
            in_full,
            out_full,
            gain_row,
            features,
            pair_sum,
            pair_spread,
        )
        in_blocks[phase] = scatter_units(in_total)
        out_blocks[phase] = scatter_units(out_total)
        returned = swap_section(result[1])
        outputs = lax.dynamic_update_slice(
            outputs, result[0], (sent_slots[phase], 0, own * part)
        )
        outputs = lax.dynamic_update_slice(
            outputs, returned, (sent_slots[phase], 0, other * part)
        )
        incoming = jnp.stack((result[1], result[0]))

    def whole(by_phase):
        kept = jnp.where(own == 1, by_phase[0], by_phase[1])
        given = jnp.where(own == 1, by_phase[1], by_phase[0]).astype(BF16)
        return ordered(kept, swap_section(given).astype(F32), own == 1, 0)

    return (whole(in_blocks)[None], whole(out_blocks)[None], outputs[None])


def any_sections(saved_inputs, cotangent, weight_in, weight_out, gain, plan):
    count = lax.axis_size("section")
    own = lax.axis_index("section")
    stored = saved_inputs[0]
    slots, tokens, width = stored.shape
    half, part = slots // 2, width // count
    features = width * lax.axis_size("mp")
    units = weight_in.shape[-1]

    def split_columns(array):
        return jnp.moveaxis(array.reshape(array.shape[:-1] + (count, part)), -2, 0)

    def moved(array):
        return lax.all_to_all(array, "section", 0, 0)

    inputs = moved(split_columns(stored))
    ins = moved(weight_in[0].reshape(count, part, units))
    outs = moved(weight_out[0].reshape(count, part, units))
    gains = pick(split_columns(gain), own, 0)
    top = lax.dynamic_slice_in_dim(cotangent, own * part, part, 2)
    incoming = jnp.stack([pick(top, plan[i], 0) for i in range(slots)])
    incoming = incoming.reshape(2, half, tokens, part)
    results = [[None, None] for _ in range(count)]
    in_blocks = [None] * count
    out_blocks = [None] * count
    for phase in range(count):
        group = count - 1 - phase
        result, in_total, out_total = run_phase(
            jnp.stack((inputs[group, :half], inputs[phase, half:])),
            incoming,
            gather_units(ins[group]),
            gather_units(outs[group]),
            gains[group],
            features,
            any_sum,
            lambda block: any_spread(block, 2, half, tokens),
        )
        in_blocks[group] = scatter_units(in_total)
        out_blocks[group] = scatter_units(out_total)
        results[group][0] = result[0]
        results[phase][1] = result[1]
        incoming = result

    def whole(blocks):
        return moved(jnp.stack(blocks).astype(BF16)).astype(F32).reshape(width, units)

    outputs = moved(jnp.stack([jnp.concatenate(pair) for pair in results]))
    outputs = jnp.moveaxis(outputs, 0, -2).reshape(stored.shape)
    return (whole(in_blocks)[None], whole(out_blocks)[None], outputs[None])


def solution(mesh):
    in_specs = (
        P("section", None, "dp", "mp"),
        P(None, "dp", "mp"),
        P("section", "mp", "dp"),
        P("section", "mp", "dp"),
        P(None, "mp"),
        P(),
    )
    out_specs = (P("section", "mp", "dp"), P("section", "mp", "dp"), P("section", None, "dp", "mp"))
    paired = mesh.shape["section"] == 2 and mesh.shape["mp"] == 4
    return jax.shard_map(
        two_sections if paired else any_sections,
        mesh=mesh,
        in_specs=in_specs,
        out_specs=out_specs,
        check_vma=False,
    )
```

```python
import jax
import jax.numpy as jnp
from jax import lax
from jax.experimental import pallas as pl
from jax.experimental.pallas import tpu as pltpu
from jax.sharding import PartitionSpec as P

EPS = 1e-05
F32 = jnp.float32
BF16 = jnp.bfloat16
PAD = 128


def rotate(block, shift):
    count = lax.axis_size("dp")
    return lax.ppermute(block, "dp", [(i, (i + shift) % count) for i in range(count)])


def gather_units(block):
    count = lax.axis_size("dp")
    return jnp.concatenate([block] + [rotate(block, -k) for k in range(1, count)], axis=-1)


def scatter_units(total):
    count = lax.axis_size("dp")
    width = total.shape[-1] // count
    parts = total.astype(BF16)
    kept = total[..., :width].astype(F32)
    for k in range(1, count):
        kept = kept + rotate(parts[..., k * width : (k + 1) * width], k).astype(F32)
    return kept


def swap_section(block):
    return lax.ppermute(block, "section", [(0, 1), (1, 0)])


def swap_core(block):
    return lax.ppermute(block, "mp", [(i, i ^ 1) for i in range(4)])


def swap_chip(block):
    return lax.ppermute(block, "mp", [(i, i ^ 2) for i in range(4)])


def swap_both(block):
    return lax.ppermute(block, ("section", "mp"), [(i, i ^ 6) for i in range(8)])


def after(array, *others):
    return lax.optimization_barrier((array,) + others)[0]


CORE, CHIP, SECTION, OWN, PLAN = 0, 1, 2, 3, 5
STEPS = 4
VMEM_BYTES = 48 * 1024 * 1024


def step_place():
    step = pl.program_id(0)
    return step, 1 - step // 2, step % 2


def slot_at(place, a, b):
    return 2 * (place[CHIP] ^ a) + (place[CORE] ^ b)


def join_units(step, parts, whole):
    @pl.when(step == 0)
    def _():
        for k, part in enumerate(parts):
            whole[:, k * part.shape[1] : (k + 1) * part.shape[1]] = part[...]


def join_slots(step, parts, whole):
    @pl.when(step == 0)
    def _():
        for k in range(4):
            whole[0, k // 2, k % 2] = parts[k][...]
        whole[1] = parts[4][...]


def load_set(place, refs, rows):
    step, b, which = step_place()
    tokens = refs[0].shape[1]
    for k in range(2):

        @pl.when(which == k)
        def _(k=k):
            for a in range(2):
                rows[a * tokens : (a + 1) * tokens] = refs[k][slot_at(place, a, b)]


def load_top(phase, place, top, rows):
    step, b, which = step_place()
    tokens, half = top.shape[1], top.shape[0] // 2
    for a in range(2):
        slot = half * (place[OWN + phase] ^ which) + slot_at(place, a, b)
        rows[a * tokens : (a + 1) * tokens] = top[place[PLAN + slot]]


def put_partial(value, sent, kept, step, which):
    value = value.astype(BF16).reshape(sent.shape[1:])

    @pl.when(step < 2)
    def _():
        sent[which] = value

    @pl.when(step >= 2)
    def _():
        kept[which] = value


def hidden_kernel(group, place, own, received, gain, w0, w1, w2, w3, sent, kept, weights, rows):
    step, b, which = step_place()
    join_units(step, (w0, w1, w2, w3), weights)
    load_set(place, (own, received), rows)
    wide = rows[...].astype(F32)
    normed = (wide * gain[group : group + 1, :]).astype(BF16)
    part = jnp.dot(normed, weights[...], preferred_element_type=F32)
    squares = jnp.sum(wide * wide, axis=1, keepdims=True)
    packed = jnp.concatenate((part, jnp.broadcast_to(squares, (part.shape[0], PAD))), axis=1)
    put_partial(packed, sent, kept, step, which)


def top_kernel(phase, place, top, w0, w1, w2, w3, sent, kept, weights, rows):
    step, b, which = step_place()
    join_units(step, (w0, w1, w2, w3), weights)
    load_top(phase, place, top, rows)
    part = jnp.dot(rows[...], weights[...], preferred_element_type=F32)
    put_partial(part, sent, kept, step, which)


def back_step(group, place, own, received, gain, spread, weights, rows, incoming):
    step, b, which = step_place()
    load_set(place, (own, received), rows)
    units = weights.shape[1]
    packed = spread[b, which].reshape(rows.shape[0], units + PAD)
    back = lax.dot_general(
        packed[:, :units], weights[...], (((1,), (1,)), ((), ())), preferred_element_type=F32
    )
    factor = packed[:, units : units + 1].astype(F32)
    result = (
        incoming.astype(F32)
        + gain[group : group + 1, :] * back
        - factor * rows[...].astype(F32)
    )
    return result.astype(BF16)


def put_result(place, result, results):
    step, b, which = step_place()
    tokens = result.shape[0] // 2
    for k in range(2):

        @pl.when(which == k)
        def _(k=k):
            for a in range(2):
                results[k][slot_at(place, a, b)] = result[a * tokens : (a + 1) * tokens]


def first_back_kernel(
    group, place, own, received, gain, top, p0, p1, p2, p3, p4, w0, w1, w2, w3, v0, v1, v2, v3,
    result0, result1, sent, kept, weights, outward, spread, rows, grads,
):
    step, b, which = step_place()
    join_units(step, (w0, w1, w2, w3), weights)
    join_units(step, (v0, v1, v2, v3), outward)
    join_slots(step, (p0, p1, p2, p3, p4), spread)
    load_top(0, place, top, grads)
    result = back_step(group, place, own, received, gain, spread, weights, rows, grads[...])
    put_result(place, result, (result0, result1))
    part = jnp.dot(result, outward[...], preferred_element_type=F32)
    put_partial(part, sent, kept, step, 1 - which)


def last_back_kernel(
    group, place, own, received, gain, in0, in1, p0, p1, p2, p3, p4, w0, w1, w2, w3,
    result0, result1, weights, spread, rows, grads,
):
    step, b, which = step_place()
    join_units(step, (w0, w1, w2, w3), weights)
    join_slots(step, (p0, p1, p2, p3, p4), spread)
    load_set(place, (in0, in1), grads)
    result = back_step(group, place, own, received, gain, spread, weights, rows, grads[...])
    put_result(place, result, (result0, result1))


def add_grad(step, total, units, rows):
    part = lax.dot_general(units, rows, (((0,), (0,)), ((), ())), preferred_element_type=F32)

    @pl.when(step == 0)
    def _():
        total[...] = part

    @pl.when(step > 0)
    def _():
        total[...] += part


def put_grad(step, total, kept, parts):
    @pl.when(step == STEPS - 1)
    def _():
        height = kept.shape[0]
        kept[...] = total[:height]
        for k, part in enumerate(parts):
            part[...] = total[(k + 1) * height : (k + 2) * height].astype(BF16)


def in_grad_kernel(
    group, place, own, received, gain, p0, p1, p2, p3, p4, kept, c1, c2, c3, total, spread, rows
):
    step, b, which = step_place()
    join_slots(step, (p0, p1, p2, p3, p4), spread)
    load_set(place, (own, received), rows)
    normed = (rows[...].astype(F32) * gain[group : group + 1, :]).astype(BF16)
    packed = spread[b, which].reshape(rows.shape[0], spread.shape[-1])
    add_grad(step, total, packed[:, : total.shape[0]], normed)
    put_grad(step, total, kept, (c1, c2, c3))


def top_grad_kernel(place, top, p0, p1, p2, p3, p4, kept, c1, c2, c3, total, spread, rows):
    step, b, which = step_place()
    join_slots(step, (p0, p1, p2, p3, p4), spread)
    load_top(0, place, top, rows)
    packed = spread[b, which].reshape(rows.shape[0], spread.shape[-1])
    add_grad(step, total, packed, rows[...])
    put_grad(step, total, kept, (c1, c2, c3))


def out_grad_kernel(place, in0, in1, p0, p1, p2, p3, p4, kept, c1, c2, c3, total, spread, rows):
    step, b, which = step_place()
    join_slots(step, (p0, p1, p2, p3, p4), spread)
    load_set(place, (in0, in1), rows)
    packed = spread[b, which].reshape(rows.shape[0], spread.shape[-1])
    add_grad(step, total, packed, rows[...])
    put_grad(step, total, kept, (c1, c2, c3))


def core_sum_kernel(kept, moved, own, chip, section, both):
    def at(k):
        return kept[k // 2, k % 2].astype(F32) + moved[k // 2, k % 2].astype(F32)

    own[...] = at(0)
    chip[...] = at(1).astype(BF16)
    section[...] = at(2).astype(BF16)
    both[...] = at(3).astype(BF16)


def whole_sum(own, chip, section, both):
    return own[...] + chip[...].astype(F32) + section[...].astype(F32) + both[...].astype(F32)


def active_kernel(features, own, chip, section, both, hidden, activated):
    total = whole_sum(own, chip, section, both)
    hidden[...] = total
    units = activated.shape[1]
    terms = row_terms(total[:, :units], total[:, units : units + 1], features)
    activated[...] = terms[3]


def unit_kernel(features, hidden, own, chip, section, both, packed):
    units = own.shape[1]
    unit_sums, square_sums = hidden[:, :units], hidden[:, units : units + 1]
    inverse_rms, hidden_pre, sigma, _ = row_terms(unit_sums, square_sums, features)
    scaled_grad, factor = unit_terms(
        whole_sum(own, chip, section, both), unit_sums, inverse_rms, hidden_pre, sigma, features
    )
    packed[:, :units] = scaled_grad
    packed[:, units:] = jnp.broadcast_to(factor, (factor.shape[0], PAD)).astype(BF16)


def call(kernel, name, outs, args, scratch=(), specs=None, place=None, flops=0):
    size = sum(a.size * a.dtype.itemsize for a in args)
    size += sum(o.size * o.dtype.itemsize for o in outs)
    cost = pl.CostEstimate(flops=flops, bytes_accessed=size, transcendentals=0)
    params = pltpu.CompilerParams(vmem_limit_bytes=VMEM_BYTES)
    if place is None:
        return pl.pallas_call(
            kernel, out_shape=outs, compiler_params=params, cost_estimate=cost, name=name
        )(*args)

    def whole(shape):
        return pl.BlockSpec(shape, lambda i, s: (0,) * len(shape))

    specs = specs or {}
    return pl.pallas_call(
        kernel,
        out_shape=outs,
        grid_spec=pltpu.PrefetchScalarGridSpec(
            num_scalar_prefetch=1,
            grid=(STEPS,),
            in_specs=[specs.get(k, whole(a.shape)) for k, a in enumerate(args)],
            out_specs=[whole(o.shape) for o in outs],
            scratch_shapes=[pltpu.VMEM(shape, dtype) for shape, dtype in scratch],
        ),
        compiler_params=params,
        cost_estimate=cost,
        name=name,
    )(place, *args)


def shape_of(shape, dtype=BF16):
    return jax.ShapeDtypeStruct(shape, dtype)


def pair_sum(sent, kept):
    moved = swap_core(sent)
    small = sent.shape[2:]
    own, chip, section, both = call(
        core_sum_kernel,
        "core_sum",
        [shape_of(small, F32)] + [shape_of(small)] * 3,
        (kept, moved),
    )
    return own, swap_chip(chip), swap_section(section), swap_both(both)


def pair_spread(block):
    parts = (block, swap_chip(block), swap_section(block), swap_both(block))
    four = jnp.stack(parts).reshape((2, 2) + block.shape)
    return parts + (swap_core(four),)


def two_sections(saved_inputs, cotangent, weight_in, weight_out, gain, plan):
    own = lax.axis_index("section")
    other = 1 - own
    mp_index = lax.axis_index("mp")
    stored = saved_inputs[0]
    slots, tokens, width = stored.shape
    half, part = slots // 2, width // 2
    features = width * lax.axis_size("mp")
    place = jnp.concatenate(
        (jnp.stack((mp_index % 2, mp_index // 2, own, other, own)).astype(jnp.int32), plan)
    )

    def rows(array, section):
        return lax.dynamic_slice_in_dim(array, section * part, part, 0)

    mine = jnp.stack((rows(weight_in[0], own), rows(weight_out[0], own)))
    moved = swap_section(jnp.stack((rows(weight_in[0], other), rows(weight_out[0], other))))

    def sent_inputs(phase):
        first = half * place[OWN + phase]
        return lax.dynamic_slice(stored, (first, 0, other * part), (half, tokens, part))

    received = [None, None]
    received[0] = swap_section(after(sent_inputs(0), moved))
    received[1] = swap_section(after(sent_inputs(1), received[0]))

    def unit_parts(block):
        count = lax.axis_size("dp")
        return (block,) + tuple(rotate(block, -k) for k in range(1, count))

    in_parts, out_parts = [], []
    for phase in range(2):
        held = jnp.where(own == 1 - phase, mine, moved)
        in_parts.append(unit_parts(held[0]))
        out_parts.append(unit_parts(held[1]))
    units = 4 * mine.shape[-1]
    rows2 = 2 * tokens
    gain_spec = pl.BlockSpec((2, part), lambda i, s: (0, s[SECTION]))
    top_spec = pl.BlockSpec((slots, tokens, part), lambda i, s: (0, 0, s[SECTION]))
    partial_shapes = [shape_of((2, 2, tokens, units))] * 2
    hidden_shapes = [shape_of((2, 2, tokens, units + PAD))] * 2
    set_shape = shape_of((half, tokens, part))
    weight_scratch = ((part, units), BF16)
    rows_scratch = ((rows2, part), BF16)
    spread_scratch = ((2, 2, 2, tokens, units + PAD), BF16)
    act_scratch = ((2, 2, 2, tokens, units), BF16)
    grad_scratch = ((units, part), F32)
    grad_shapes = [shape_of((units // 4, part), F32)] + [shape_of((units // 4, part))] * 3
    one_dot = 2 * slots * tokens * part * units

    def own_spec(phase):
        return pl.BlockSpec(
            (half, tokens, part), lambda i, s: (s[OWN + phase], 0, s[SECTION])
        )

    def bind(kernel, *first):
        def bound(*refs):
            kernel(*first, *refs)

        return bound

    def hidden_part(phase):
        return call(
            bind(hidden_kernel, 1 - phase),
            "hidden_part",
            hidden_shapes,
            (stored, received[phase], gain) + in_parts[phase],
            [weight_scratch, rows_scratch],
            {0: own_spec(phase), 2: gain_spec},
            place,
            one_dot,
        )

    def hidden_terms(sums):
        return call(
            bind(active_kernel, features),
            "activated",
            [shape_of((tokens, units + PAD), F32), shape_of((tokens, units))],
            sums,
        )

    def unit_grad_terms(hidden, sums):
        return call(
            bind(unit_kernel, features),
            "unit_grads",
            [shape_of((tokens, units + PAD))],
            (hidden,) + sums,
        )[0]

    def in_grad(phase, scaled):
        return call(
            bind(in_grad_kernel, 1 - phase),
            "in_grad",
            grad_shapes,
            (stored, received[phase], gain) + scaled,
            [grad_scratch, spread_scratch, rows_scratch],
            {0: own_spec(phase), 2: gain_spec},
            place,
            one_dot,
        )

    def scatter(parts):
        total = parts[0]
        for k in range(1, 4):
            total = total + rotate(parts[k], k).astype(F32)
        return total

    hidden0, act0 = hidden_terms(pair_sum(*hidden_part(0)))
    act0 = pair_spread(act0)
    sent, kept = call(
        bind(top_kernel, 0),
        "top_part",
        partial_shapes,
        (cotangent,) + out_parts[0],
        [weight_scratch, rows_scratch],
        {0: top_spec},
        place,
        one_dot,
    )
    scaled0 = pair_spread(unit_grad_terms(hidden0, pair_sum(sent, kept)))
    result0, result1, sent, kept = call(
        bind(first_back_kernel, 1),
        "first_back",
        [set_shape, set_shape] + partial_shapes,
        (stored, received[0], gain, cotangent) + scaled0 + in_parts[0] + out_parts[1],
        [weight_scratch, weight_scratch, spread_scratch, rows_scratch, rows_scratch],
        {0: own_spec(0), 2: gain_spec, 3: top_spec},
        place,
        2 * one_dot,
    )
    in_total0 = scatter(in_grad(0, scaled0))
    out_total0 = scatter(
        call(
            top_grad_kernel,
            "top_grad",
            grad_shapes,
            (cotangent,) + act0,
            [grad_scratch, act_scratch, rows_scratch],
            {0: top_spec},
            place,
            one_dot,
        )
    )
    hidden1, act1 = hidden_terms(pair_sum(*hidden_part(1)))
    act1 = pair_spread(act1)
    out_total1 = scatter(
        call(
            out_grad_kernel,
            "out_grad",
            grad_shapes,
            (result1, result0) + act1,
            [grad_scratch, act_scratch, rows_scratch],
            None,
            place,
            one_dot,
        )
    )
    scaled1 = pair_spread(unit_grad_terms(hidden1, pair_sum(sent, kept)))
    returned0 = swap_section(after(result1, scaled1[4]))
    in_total1 = scatter(in_grad(1, scaled1))
    result2, result3 = call(
        bind(last_back_kernel, 0),
        "last_back",
        [set_shape, set_shape],
        (stored, received[1], gain, result1, result0) + scaled1 + in_parts[1],
        [weight_scratch, spread_scratch, rows_scratch, rows_scratch],
        {0: own_spec(1), 2: gain_spec},
        place,
        one_dot,
    )
    returned1 = swap_section(result3)
    outputs = jnp.zeros_like(stored)
    for phase, block, back in ((0, result0, returned0), (1, result2, returned1)):
        first = half * place[OWN + phase]
        outputs = lax.dynamic_update_slice(outputs, block, (first, 0, own * part))
        outputs = lax.dynamic_update_slice(outputs, back, (first, 0, other * part))

    def whole(total0, total1):
        kept = jnp.where(own == 1, total0, total1)
        given = jnp.where(own == 1, total1, total0).astype(BF16)
        back = swap_section(given).astype(F32)
        return jnp.where(
            own == 1,
            jnp.concatenate((back, kept), 1),
            jnp.concatenate((kept, back), 1),
        ).T

    return (whole(in_total0, in_total1)[None], whole(out_total0, out_total1)[None], outputs[None])


def pick(array, index, axis):
    return lax.dynamic_index_in_dim(array, index, axis, keepdims=False)


def any_sum(partial):
    sets, slots, tokens, width = partial.shape
    count = lax.axis_size("section") * lax.axis_size("mp")
    rows = partial.astype(BF16).reshape(count, sets * slots * tokens // count, width)
    moved = lax.all_to_all(rows, ("section", "mp"), 0, 0)
    return jnp.sum(moved.astype(F32), axis=0)


def any_spread(block, sets, slots, tokens):
    whole = lax.all_gather(block, ("section", "mp"), axis=0, tiled=True)
    return whole.reshape(sets, slots, tokens, block.shape[-1])


def row_terms(unit_sums, square_sums, features):
    inverse_rms = lax.rsqrt(square_sums / features + EPS)
    hidden_pre = inverse_rms * unit_sums
    sigma = jax.nn.sigmoid(hidden_pre)
    activated = (hidden_pre * sigma).astype(BF16)
    return inverse_rms, hidden_pre, sigma, activated


def unit_terms(unit_grads, unit_sums, inverse_rms, hidden_pre, sigma, features):
    grad_hidden = unit_grads * sigma * (1.0 + hidden_pre * (1.0 - sigma))
    scaled_grad = (inverse_rms * grad_hidden).astype(BF16)
    rms_term = jnp.sum(grad_hidden * unit_sums, axis=-1, keepdims=True)
    factor = inverse_rms**3 / features * rms_term
    return scaled_grad, factor


def project(rows, weights):
    return jnp.einsum("jktd,de->jkte", rows, weights, preferred_element_type=F32)


def accumulate(rows, units):
    return jnp.einsum("jktd,jkte->de", rows, units, preferred_element_type=F32)


def run_phase(stored, incoming, in_full, out_full, gain_row, features, sum_units, spread_units):
    units = in_full.shape[-1]
    wide = stored.astype(F32)
    normed = (wide * gain_row).astype(BF16)
    squares = jnp.sum(wide * wide, axis=-1, keepdims=True)
    part = project(normed, in_full)
    packed = jnp.concatenate((part, jnp.broadcast_to(squares, part.shape[:-1] + (PAD,))), axis=-1)
    hidden = sum_units(packed)
    unit_sums, square_sums = hidden[:, :units], hidden[:, units : units + 1]
    inverse_rms, hidden_pre, sigma, activated = row_terms(unit_sums, square_sums, features)
    activated = spread_units(activated)
    unit_grads = sum_units(project(incoming, out_full))
    scaled_grad, factor = unit_terms(
        unit_grads, unit_sums, inverse_rms, hidden_pre, sigma, features
    )
    factor = jnp.broadcast_to(factor.astype(BF16), (factor.shape[0], PAD))
    spread = spread_units(jnp.concatenate((scaled_grad, factor), axis=-1))
    scaled_grad, factor = spread[..., :units], spread[..., units : units + 1].astype(F32)
    back = jnp.einsum("jkte,de->jktd", scaled_grad, in_full, preferred_element_type=F32)
    result = (incoming.astype(F32) + gain_row * back - factor * wide).astype(BF16)
    return result, accumulate(normed, scaled_grad), accumulate(incoming, activated)


def any_sections(saved_inputs, cotangent, weight_in, weight_out, gain, plan):
    count = lax.axis_size("section")
    own = lax.axis_index("section")
    stored = saved_inputs[0]
    slots, tokens, width = stored.shape
    half, part = slots // 2, width // count
    features = width * lax.axis_size("mp")
    units = weight_in.shape[-1]

    def split_columns(array):
        return jnp.moveaxis(array.reshape(array.shape[:-1] + (count, part)), -2, 0)

    def moved(array):
        return lax.all_to_all(array, "section", 0, 0)

    inputs = moved(split_columns(stored))
    ins = moved(weight_in[0].reshape(count, part, units))
    outs = moved(weight_out[0].reshape(count, part, units))
    gains = pick(split_columns(gain), own, 0)
    top = lax.dynamic_slice_in_dim(cotangent, own * part, part, 2)
    incoming = jnp.stack([pick(top, plan[i], 0) for i in range(slots)])
    incoming = incoming.reshape(2, half, tokens, part)
    results = [[None, None] for _ in range(count)]
    in_blocks = [None] * count
    out_blocks = [None] * count
    for phase in range(count):
        group = count - 1 - phase
        result, in_total, out_total = run_phase(
            jnp.stack((inputs[group, :half], inputs[phase, half:])),
            incoming,
            gather_units(ins[group]),
            gather_units(outs[group]),
            gains[group],
            features,
            any_sum,
            lambda block: any_spread(block, 2, half, tokens),
        )
        in_blocks[group] = scatter_units(in_total)
        out_blocks[group] = scatter_units(out_total)
        results[group][0] = result[0]
        results[phase][1] = result[1]
        incoming = result

    def whole(blocks):
        return moved(jnp.stack(blocks).astype(BF16)).astype(F32).reshape(width, units)

    outputs = moved(jnp.stack([jnp.concatenate(pair) for pair in results]))
    outputs = jnp.moveaxis(outputs, 0, -2).reshape(stored.shape)
    return (whole(in_blocks)[None], whole(out_blocks)[None], outputs[None])


def solution(mesh):
    in_specs = (
        P("section", None, "dp", "mp"),
        P(None, "dp", "mp"),
        P("section", "mp", "dp"),
        P("section", "mp", "dp"),
        P(None, "mp"),
        P(),
    )
    out_specs = (P("section", "mp", "dp"), P("section", "mp", "dp"), P("section", None, "dp", "mp"))
    paired = mesh.shape["section"] == 2 and mesh.shape["mp"] == 4
    return jax.shard_map(
        two_sections if paired else any_sections,
        mesh=mesh,
        in_specs=in_specs,
        out_specs=out_specs,
        check_vma=False,
    )
```

```python
import jax
import jax.numpy as jnp
from jax import lax
from jax.experimental import pallas as pl
from jax.experimental.pallas import tpu as pltpu
from jax.sharding import PartitionSpec as P

EPS = 1e-05
F32 = jnp.float32
BF16 = jnp.bfloat16
PAD = 128


def rotate(block, shift):
    count = lax.axis_size("dp")
    return lax.ppermute(block, "dp", [(i, (i + shift) % count) for i in range(count)])


def gather_units(block):
    count = lax.axis_size("dp")
    return jnp.concatenate([block] + [rotate(block, -k) for k in range(1, count)], axis=-1)


def scatter_units(total):
    count = lax.axis_size("dp")
    width = total.shape[-1] // count
    parts = total.astype(BF16)
    kept = total[..., :width].astype(F32)
    for k in range(1, count):
        kept = kept + rotate(parts[..., k * width : (k + 1) * width], k).astype(F32)
    return kept


def trade_inner(block):
    return lax.ppermute(block, "dp", [(1, 2), (2, 1)])


def trade_outward(block):
    return lax.ppermute(block, "dp", [(2, 3), (1, 0)])


def trade_inward(block):
    return lax.ppermute(block, "dp", [(3, 2), (0, 1)])


def swap_section(block):
    return lax.ppermute(block, "section", [(0, 1), (1, 0)])


def swap_core(block):
    return lax.ppermute(block, "mp", [(i, i ^ 1) for i in range(4)])


def swap_chip(block):
    return lax.ppermute(block, "mp", [(i, i ^ 2) for i in range(4)])


def swap_both(block):
    return lax.ppermute(block, ("section", "mp"), [(i, i ^ 6) for i in range(8)])


def after(array, *others):
    return lax.optimization_barrier((array,) + others)[0]


CORE, CHIP, SECTION, OWN, PLAN = 0, 1, 2, 3, 5
STEPS = 4
VMEM_BYTES = 48 * 1024 * 1024


def step_place():
    step = pl.program_id(0)
    return step, 1 - step // 2, step % 2


def slot_at(place, a, b):
    return 2 * (place[CHIP] ^ a) + (place[CORE] ^ b)


def join_units(step, parts, whole):
    @pl.when(step == 0)
    def _():
        for k, part in enumerate(parts):
            whole[:, k * part.shape[1] : (k + 1) * part.shape[1]] = part[...]


def join_slots(step, parts, whole):
    @pl.when(step == 0)
    def _():
        for k in range(4):
            whole[0, k // 2, k % 2] = parts[k][...]
        whole[1] = parts[4][...]


def load_set(place, refs, rows):
    step, b, which = step_place()
    tokens = refs[0].shape[1]
    for k in range(2):

        @pl.when(which == k)
        def _(k=k):
            for a in range(2):
                rows[a * tokens : (a + 1) * tokens] = refs[k][slot_at(place, a, b)]


def load_top(phase, place, top, rows):
    step, b, which = step_place()
    tokens, half = top.shape[1], top.shape[0] // 2
    for a in range(2):
        slot = half * (place[OWN + phase] ^ which) + slot_at(place, a, b)
        rows[a * tokens : (a + 1) * tokens] = top[place[PLAN + slot]]


def put_partial(value, sent, kept, step, which):
    value = value.astype(BF16).reshape(sent.shape[1:])

    @pl.when(step < 2)
    def _():
        sent[which] = value

    @pl.when(step >= 2)
    def _():
        kept[which] = value


def hidden_kernel(group, place, own, received, gain, w0, w1, w2, w3, sent, kept, weights, rows):
    step, b, which = step_place()
    join_units(step, (w0.at[0], w1.at[0], w2.at[0], w3.at[0]), weights)
    load_set(place, (own, received), rows)
    wide = rows[...].astype(F32)
    normed = (wide * gain[group : group + 1, :]).astype(BF16)
    part = jnp.dot(normed, weights[...], preferred_element_type=F32)
    squares = jnp.sum(wide * wide, axis=1, keepdims=True)
    packed = jnp.concatenate((part, jnp.broadcast_to(squares, (part.shape[0], PAD))), axis=1)
    put_partial(packed, sent, kept, step, which)


def first_part_kernel(
    group, place, own, received, gain, top, w0, w1, w2, w3, sent, kept, weights, outward, rows
):
    step, b, which = step_place()
    join_units(step, (w0.at[0], w1.at[0], w2.at[0], w3.at[0]), weights)
    join_units(step, (w0.at[1], w1.at[1], w2.at[1], w3.at[1]), outward)
    load_set(place, (own, received), rows)
    wide = rows[...].astype(F32)
    normed = (wide * gain[group : group + 1, :]).astype(BF16)
    part = jnp.dot(normed, weights[...], preferred_element_type=F32)
    squares = jnp.sum(wide * wide, axis=1, keepdims=True)
    load_top(0, place, top, rows)
    top_part = jnp.dot(rows[...], outward[...], preferred_element_type=F32)
    padded = jnp.broadcast_to(squares, (part.shape[0], PAD))
    put_partial(jnp.concatenate((part, padded, top_part), axis=1), sent, kept, step, which)


def back_step(group, place, own, received, gain, spread, weights, rows, incoming):
    step, b, which = step_place()
    load_set(place, (own, received), rows)
    units = weights.shape[1]
    packed = spread[b, which].reshape(rows.shape[0], units + PAD)
    back = lax.dot_general(
        packed[:, :units], weights[...], (((1,), (1,)), ((), ())), preferred_element_type=F32
    )
    factor = packed[:, units : units + 1].astype(F32)
    result = (
        incoming.astype(F32)
        + gain[group : group + 1, :] * back
        - factor * rows[...].astype(F32)
    )
    return result.astype(BF16)


def put_result(place, result, results):
    step, b, which = step_place()
    tokens = result.shape[0] // 2
    for k in range(2):

        @pl.when(which == k)
        def _(k=k):
            for a in range(2):
                results[k][slot_at(place, a, b)] = result[a * tokens : (a + 1) * tokens]


def first_back_kernel(
    group, place, own, received, gain, top, p0, p1, p2, p3, p4, w0, w1, w2, w3, v0, v1, v2, v3,
    result0, result1, sent, kept, weights, outward, spread, rows, grads,
):
    step, b, which = step_place()
    join_units(step, (w0.at[0], w1.at[0], w2.at[0], w3.at[0]), weights)
    join_units(step, (v0.at[1], v1.at[1], v2.at[1], v3.at[1]), outward)
    join_slots(step, (p0, p1, p2, p3, p4), spread)
    load_top(0, place, top, grads)
    result = back_step(group, place, own, received, gain, spread, weights, rows, grads[...])
    put_result(place, result, (result0, result1))
    part = jnp.dot(result, outward[...], preferred_element_type=F32)
    put_partial(part, sent, kept, step, 1 - which)


def last_back_kernel(
    group, place, own, received, gain, in0, in1, p0, p1, p2, p3, p4, w0, w1, w2, w3,
    result0, result1, weights, spread, rows, grads,
):
    step, b, which = step_place()
    join_units(step, (w0.at[0], w1.at[0], w2.at[0], w3.at[0]), weights)
    join_slots(step, (p0, p1, p2, p3, p4), spread)
    load_set(place, (in0, in1), grads)
    result = back_step(group, place, own, received, gain, spread, weights, rows, grads[...])
    put_result(place, result, (result0, result1))


def add_grad(step, total, units, rows):
    part = lax.dot_general(units, rows, (((0,), (0,)), ((), ())), preferred_element_type=F32)

    @pl.when(step == 0)
    def _():
        total[...] = part

    @pl.when(step > 0)
    def _():
        total[...] += part


def put_grad(step, total, kept, parts, at=0):
    @pl.when(step == STEPS - 1)
    def _():
        height = kept.shape[1]
        kept[at] = total[:height]
        for k, part in enumerate(parts):
            part[at] = total[(k + 1) * height : (k + 2) * height].astype(BF16)


def in_grad_kernel(
    group, place, own, received, gain, p0, p1, p2, p3, p4, kept, c1, c2, c3, total, spread, rows
):
    step, b, which = step_place()
    join_slots(step, (p0, p1, p2, p3, p4), spread)
    load_set(place, (own, received), rows)
    normed = (rows[...].astype(F32) * gain[group : group + 1, :]).astype(BF16)
    packed = spread[b, which].reshape(rows.shape[0], spread.shape[-1])
    add_grad(step, total, packed[:, : total.shape[0]], normed)
    put_grad(step, total, kept, (c1, c2, c3))


def first_grad_kernel(
    group, place, own, received, gain, top, p0, p1, p2, p3, p4, a0, a1, a2, a3, a4,
    kept, c1, c2, c3, total, out_total, spread, active, rows,
):
    step, b, which = step_place()
    join_slots(step, (p0, p1, p2, p3, p4), spread)
    join_slots(step, (a0, a1, a2, a3, a4), active)
    load_set(place, (own, received), rows)
    normed = (rows[...].astype(F32) * gain[group : group + 1, :]).astype(BF16)
    packed = spread[b, which].reshape(rows.shape[0], spread.shape[-1])
    add_grad(step, total, packed[:, : total.shape[0]], normed)
    load_top(0, place, top, rows)
    add_grad(step, out_total, active[b, which].reshape(rows.shape[0], active.shape[-1]), rows[...])
    put_grad(step, total, kept, (c1, c2, c3), 0)
    put_grad(step, out_total, kept, (c1, c2, c3), 1)


def out_grad_kernel(place, in0, in1, p0, p1, p2, p3, p4, kept, c1, c2, c3, total, spread, rows):
    step, b, which = step_place()
    join_slots(step, (p0, p1, p2, p3, p4), spread)
    load_set(place, (in0, in1), rows)
    packed = spread[b, which].reshape(rows.shape[0], spread.shape[-1])
    add_grad(step, total, packed, rows[...])
    put_grad(step, total, kept, (c1, c2, c3))


def core_sum_kernel(kept, moved, own, chip, section, both):
    def at(k):
        return kept[k // 2, k % 2].astype(F32) + moved[k // 2, k % 2].astype(F32)

    own[...] = at(0)
    chip[...] = at(1).astype(BF16)
    section[...] = at(2).astype(BF16)
    both[...] = at(3).astype(BF16)


def whole_sum(own, chip, section, both):
    return own[...] + chip[...].astype(F32) + section[...].astype(F32) + both[...].astype(F32)


def active_kernel(features, own, chip, section, both, hidden, activated):
    total = whole_sum(own, chip, section, both)
    hidden[...] = total
    units = activated.shape[1]
    terms = row_terms(total[:, :units], total[:, units : units + 1], features)
    activated[...] = terms[3]


def put_units(features, hidden, unit_grads, packed):
    units = unit_grads.shape[1]
    unit_sums, square_sums = hidden[:, :units], hidden[:, units : units + 1]
    inverse_rms, hidden_pre, sigma, activated = row_terms(unit_sums, square_sums, features)
    scaled_grad, factor = unit_terms(
        unit_grads, unit_sums, inverse_rms, hidden_pre, sigma, features
    )
    packed[:, :units] = scaled_grad
    packed[:, units:] = jnp.broadcast_to(factor, (factor.shape[0], PAD)).astype(BF16)
    return activated


def first_unit_kernel(features, own, chip, section, both, packed, activated):
    units = activated.shape[1]
    total = whole_sum(own, chip, section, both)
    activated[...] = put_units(features, total, total[:, units + PAD :], packed)


def unit_kernel(features, hidden, own, chip, section, both, packed):
    put_units(features, hidden, whole_sum(own, chip, section, both), packed)


def call(kernel, name, outs, args, scratch=(), specs=None, place=None, flops=0):
    size = sum(a.size * a.dtype.itemsize for a in args)
    size += sum(o.size * o.dtype.itemsize for o in outs)
    cost = pl.CostEstimate(flops=flops, bytes_accessed=size, transcendentals=0)
    params = pltpu.CompilerParams(vmem_limit_bytes=VMEM_BYTES)
    if place is None:
        return pl.pallas_call(
            kernel, out_shape=outs, compiler_params=params, cost_estimate=cost, name=name
        )(*args)

    def whole(shape):
        return pl.BlockSpec(shape, lambda i, s: (0,) * len(shape))

    specs = specs or {}
    return pl.pallas_call(
        kernel,
        out_shape=outs,
        grid_spec=pltpu.PrefetchScalarGridSpec(
            num_scalar_prefetch=1,
            grid=(STEPS,),
            in_specs=[specs.get(k, whole(a.shape)) for k, a in enumerate(args)],
            out_specs=[whole(o.shape) for o in outs],
            scratch_shapes=[pltpu.VMEM(shape, dtype) for shape, dtype in scratch],
        ),
        compiler_params=params,
        cost_estimate=cost,
        name=name,
    )(place, *args)


def shape_of(shape, dtype=BF16):
    return jax.ShapeDtypeStruct(shape, dtype)


def pair_sum(sent, kept):
    moved = swap_core(sent)
    small = sent.shape[2:]
    own, chip, section, both = call(
        core_sum_kernel,
        "core_sum",
        [shape_of(small, F32)] + [shape_of(small)] * 3,
        (kept, moved),
    )
    return own, swap_chip(chip), swap_section(section), swap_both(both)


def pair_spread(block):
    parts = (block, swap_chip(block), swap_section(block), swap_both(block))
    four = jnp.stack(parts).reshape((2, 2) + block.shape)
    return parts + (swap_core(four),)


def two_sections(saved_inputs, cotangent, weight_in, weight_out, gain, plan):
    own = lax.axis_index("section")
    other = 1 - own
    mp_index = lax.axis_index("mp")
    stored = saved_inputs[0]
    slots, tokens, width = stored.shape
    half, part = slots // 2, width // 2
    features = width * lax.axis_size("mp")
    place = jnp.concatenate(
        (jnp.stack((mp_index % 2, mp_index // 2, own, other, own)).astype(jnp.int32), plan)
    )

    def rows(array, section):
        return lax.dynamic_slice_in_dim(array, section * part, part, 0)

    mine = jnp.stack((rows(weight_in[0], own), rows(weight_out[0], own)))
    moved = swap_section(jnp.stack((rows(weight_in[0], other), rows(weight_out[0], other))))

    def sent_inputs(phase):
        first = half * place[OWN + phase]
        return lax.dynamic_slice(stored, (first, 0, other * part), (half, tokens, part))

    received = swap_section(after(jnp.stack((sent_inputs(0), sent_inputs(1))), moved))

    position = lax.axis_index("dp")

    def near(block):
        return rotate(block, 1), rotate(block, -1)

    def far(below, above):
        inner = trade_inner(jnp.where(position == 1, below, above))
        outward = trade_outward(jnp.where(position == 2, below, above))
        return inner, outward

    def joined(inner, outward):
        return jnp.where((position == 1) | (position == 2), inner, outward)

    held0 = jnp.where(own == 1, mine, moved)
    held1 = jnp.where(own == 0, mine, moved)
    below, above = near(held0)
    weights0 = (held0, above, joined(*far(below, above)), below)
    below, above = near(after(held1, below, above))
    far1 = far(below, above)
    weights1 = (held1, above, joined(*far1), below)
    units = 4 * mine.shape[-1]
    rows2 = 2 * tokens
    gain_spec = pl.BlockSpec((2, part), lambda i, s: (0, s[SECTION]))
    top_spec = pl.BlockSpec((slots, tokens, part), lambda i, s: (0, 0, s[SECTION]))
    partial_shapes = [shape_of((2, 2, tokens, units))] * 2
    hidden_shapes = [shape_of((2, 2, tokens, units + PAD))] * 2
    set_shape = shape_of((half, tokens, part))
    weight_scratch = ((part, units), BF16)
    rows_scratch = ((rows2, part), BF16)
    spread_scratch = ((2, 2, 2, tokens, units + PAD), BF16)
    act_scratch = ((2, 2, 2, tokens, units), BF16)
    grad_scratch = ((units, part), F32)
    grad_shapes = [shape_of((1, units // 4, part), F32)] + [shape_of((1, units // 4, part))] * 3
    one_dot = 2 * slots * tokens * part * units

    both_grad_shapes = [shape_of((2, units // 4, part), F32)] + [
        shape_of((2, units // 4, part))
    ] * 3
    first_shapes = [shape_of((2, 2, tokens, 2 * units + PAD))] * 2

    def received_spec(phase):
        return pl.BlockSpec((None, half, tokens, part), lambda i, s: (phase, 0, 0, 0))

    def own_spec(phase):
        return pl.BlockSpec(
            (half, tokens, part), lambda i, s: (s[OWN + phase], 0, s[SECTION])
        )

    def bind(kernel, *first):
        def bound(*refs):
            kernel(*first, *refs)

        return bound

    def scatter(parts):
        kept, next_part, far_part, last_part = parts
        inner, inward = trade_inner(far_part), trade_inward(far_part)
        onward = jnp.where(position == 2, inner, inward)
        backward = jnp.where(position == 1, inner, inward)
        middle = (position == 1) | (position == 2)
        zero = jnp.zeros((), F32)
        forth = next_part.astype(F32) + jnp.where(middle, onward.astype(F32), zero)
        back = last_part.astype(F32) + jnp.where(middle, backward.astype(F32), zero)
        return kept, rotate(forth.astype(BF16), 1), rotate(back.astype(BF16), -1)

    def total(parts):
        return parts[0] + parts[1].astype(F32) + parts[2].astype(F32)

    sent, kept = call(
        bind(first_part_kernel, 1),
        "first_part",
        first_shapes,
        (stored, received, gain, cotangent) + weights0,
        [weight_scratch, weight_scratch, rows_scratch],
        {0: own_spec(0), 1: received_spec(0), 2: gain_spec, 3: top_spec},
        place,
        2 * one_dot,
    )
    scaled0, act0 = call(
        bind(first_unit_kernel, features),
        "first_units",
        [shape_of((tokens, units + PAD)), shape_of((tokens, units))],
        pair_sum(sent, kept),
    )
    scaled0 = pair_spread(scaled0)
    act0 = pair_spread(act0)
    result0, result1, sent, kept = call(
        bind(first_back_kernel, 1),
        "first_back",
        [set_shape, set_shape] + partial_shapes,
        (stored, received, gain, cotangent) + scaled0 + weights0 + weights1,
        [weight_scratch, weight_scratch, spread_scratch, rows_scratch, rows_scratch],
        {0: own_spec(0), 1: received_spec(0), 2: gain_spec, 3: top_spec},
        place,
        2 * one_dot,
    )
    hidden1, act1 = call(
        bind(active_kernel, features),
        "activated",
        [shape_of((tokens, units + PAD), F32), shape_of((tokens, units))],
        pair_sum(
            *call(
                bind(hidden_kernel, 0),
                "hidden_part",
                hidden_shapes,
                (stored, received, gain) + weights1,
                [weight_scratch, rows_scratch],
                {0: own_spec(1), 1: received_spec(1), 2: gain_spec},
                place,
                one_dot,
            )
        ),
    )
    act1 = pair_spread(act1)
    grads0 = call(
        bind(first_grad_kernel, 1),
        "first_grads",
        both_grad_shapes,
        (stored, received, gain, cotangent) + scaled0 + act0,
        [grad_scratch, grad_scratch, spread_scratch, act_scratch, rows_scratch],
        {0: own_spec(0), 1: received_spec(0), 2: gain_spec, 3: top_spec},
        place,
        2 * one_dot,
    )
    sums = pair_sum(sent, kept)
    scaled1 = call(
        bind(unit_kernel, features),
        "unit_grads",
        [shape_of((tokens, units + PAD))],
        (after(hidden1, grads0[0]),) + sums,
    )[0]
    scaled1 = pair_spread(scaled1)
    totals0 = scatter(grads0)
    out_totals1 = scatter(
        call(
            out_grad_kernel,
            "out_grad",
            grad_shapes,
            (result1, result0) + act1,
            [grad_scratch, act_scratch, rows_scratch],
            None,
            place,
            one_dot,
        )
    )
    returned0 = swap_section(after(result1, scaled1[1]))
    in_grads1 = call(
        bind(in_grad_kernel, 0),
        "in_grad",
        grad_shapes,
        (stored, received, gain) + scaled1,
        [grad_scratch, spread_scratch, rows_scratch],
        {0: own_spec(1), 1: received_spec(1), 2: gain_spec},
        place,
        one_dot,
    )
    in_totals1 = scatter(in_grads1)
    result2, result3 = call(
        bind(last_back_kernel, 0),
        "last_back",
        [set_shape, set_shape],
        (stored, received, gain, result1, after(result0, in_grads1[0])) + scaled1 + weights1,
        [weight_scratch, spread_scratch, rows_scratch, rows_scratch],
        {0: own_spec(1), 1: received_spec(1), 2: gain_spec},
        place,
        one_dot,
    )
    returned1 = swap_section(result3)
    total0 = total(totals0)
    out_total1 = total(out_totals1)[0]
    in_total1 = total(after(in_totals1, result3))[0]
    in_total0, out_total0 = total0[0], total0[1]
    outputs = jnp.zeros_like(stored)
    for phase, block, back in ((0, result0, returned0), (1, result2, returned1)):
        first = half * place[OWN + phase]
        outputs = lax.dynamic_update_slice(outputs, block, (first, 0, own * part))
        outputs = lax.dynamic_update_slice(outputs, back, (first, 0, other * part))

    def whole(total0, total1):
        kept = jnp.where(own == 1, total0, total1)
        given = jnp.where(own == 1, total1, total0).astype(BF16)
        back = swap_section(given).astype(F32)
        return jnp.where(
            own == 1,
            jnp.concatenate((back, kept), 1),
            jnp.concatenate((kept, back), 1),
        ).T

    return (whole(in_total0, in_total1)[None], whole(out_total0, out_total1)[None], outputs[None])


def pick(array, index, axis):
    return lax.dynamic_index_in_dim(array, index, axis, keepdims=False)


def any_sum(partial):
    sets, slots, tokens, width = partial.shape
    count = lax.axis_size("section") * lax.axis_size("mp")
    rows = partial.astype(BF16).reshape(count, sets * slots * tokens // count, width)
    moved = lax.all_to_all(rows, ("section", "mp"), 0, 0)
    return jnp.sum(moved.astype(F32), axis=0)


def any_spread(block, sets, slots, tokens):
    whole = lax.all_gather(block, ("section", "mp"), axis=0, tiled=True)
    return whole.reshape(sets, slots, tokens, block.shape[-1])


def row_terms(unit_sums, square_sums, features):
    inverse_rms = lax.rsqrt(square_sums / features + EPS)
    hidden_pre = inverse_rms * unit_sums
    sigma = jax.nn.sigmoid(hidden_pre)
    activated = (hidden_pre * sigma).astype(BF16)
    return inverse_rms, hidden_pre, sigma, activated


def unit_terms(unit_grads, unit_sums, inverse_rms, hidden_pre, sigma, features):
    grad_hidden = unit_grads * sigma * (1.0 + hidden_pre * (1.0 - sigma))
    scaled_grad = (inverse_rms * grad_hidden).astype(BF16)
    rms_term = jnp.sum(grad_hidden * unit_sums, axis=-1, keepdims=True)
    factor = inverse_rms**3 / features * rms_term
    return scaled_grad, factor


def project(rows, weights):
    return jnp.einsum("jktd,de->jkte", rows, weights, preferred_element_type=F32)


def accumulate(rows, units):
    return jnp.einsum("jktd,jkte->de", rows, units, preferred_element_type=F32)


def run_phase(stored, incoming, in_full, out_full, gain_row, features, sum_units, spread_units):
    units = in_full.shape[-1]
    wide = stored.astype(F32)
    normed = (wide * gain_row).astype(BF16)
    squares = jnp.sum(wide * wide, axis=-1, keepdims=True)
    part = project(normed, in_full)
    packed = jnp.concatenate((part, jnp.broadcast_to(squares, part.shape[:-1] + (PAD,))), axis=-1)
    hidden = sum_units(packed)
    unit_sums, square_sums = hidden[:, :units], hidden[:, units : units + 1]
    inverse_rms, hidden_pre, sigma, activated = row_terms(unit_sums, square_sums, features)
    activated = spread_units(activated)
    unit_grads = sum_units(project(incoming, out_full))
    scaled_grad, factor = unit_terms(
        unit_grads, unit_sums, inverse_rms, hidden_pre, sigma, features
    )
    factor = jnp.broadcast_to(factor.astype(BF16), (factor.shape[0], PAD))
    spread = spread_units(jnp.concatenate((scaled_grad, factor), axis=-1))
    scaled_grad, factor = spread[..., :units], spread[..., units : units + 1].astype(F32)
    back = jnp.einsum("jkte,de->jktd", scaled_grad, in_full, preferred_element_type=F32)
    result = (incoming.astype(F32) + gain_row * back - factor * wide).astype(BF16)
    return result, accumulate(normed, scaled_grad), accumulate(incoming, activated)


def any_sections(saved_inputs, cotangent, weight_in, weight_out, gain, plan):
    count = lax.axis_size("section")
    own = lax.axis_index("section")
    stored = saved_inputs[0]
    slots, tokens, width = stored.shape
    half, part = slots // 2, width // count
    features = width * lax.axis_size("mp")
    units = weight_in.shape[-1]

    def split_columns(array):
        return jnp.moveaxis(array.reshape(array.shape[:-1] + (count, part)), -2, 0)

    def moved(array):
        return lax.all_to_all(array, "section", 0, 0)

    inputs = moved(split_columns(stored))
    ins = moved(weight_in[0].reshape(count, part, units))
    outs = moved(weight_out[0].reshape(count, part, units))
    gains = pick(split_columns(gain), own, 0)
    top = lax.dynamic_slice_in_dim(cotangent, own * part, part, 2)
    incoming = jnp.stack([pick(top, plan[i], 0) for i in range(slots)])
    incoming = incoming.reshape(2, half, tokens, part)
    results = [[None, None] for _ in range(count)]
    in_blocks = [None] * count
    out_blocks = [None] * count
    for phase in range(count):
        group = count - 1 - phase
        result, in_total, out_total = run_phase(
            jnp.stack((inputs[group, :half], inputs[phase, half:])),
            incoming,
            gather_units(ins[group]),
            gather_units(outs[group]),
            gains[group],
            features,
            any_sum,
            lambda block: any_spread(block, 2, half, tokens),
        )
        in_blocks[group] = scatter_units(in_total)
        out_blocks[group] = scatter_units(out_total)
        results[group][0] = result[0]
        results[phase][1] = result[1]
        incoming = result

    def whole(blocks):
        return moved(jnp.stack(blocks).astype(BF16)).astype(F32).reshape(width, units)

    outputs = moved(jnp.stack([jnp.concatenate(pair) for pair in results]))
    outputs = jnp.moveaxis(outputs, 0, -2).reshape(stored.shape)
    return (whole(in_blocks)[None], whole(out_blocks)[None], outputs[None])


def solution(mesh):
    in_specs = (
        P("section", None, "dp", "mp"),
        P(None, "dp", "mp"),
        P("section", "mp", "dp"),
        P("section", "mp", "dp"),
        P(None, "mp"),
        P(),
    )
    out_specs = (P("section", "mp", "dp"), P("section", "mp", "dp"), P("section", None, "dp", "mp"))
    paired = mesh.shape["section"] == 2 and mesh.shape["mp"] == 4
    return jax.shard_map(
        two_sections if paired else any_sections,
        mesh=mesh,
        in_specs=in_specs,
        out_specs=out_specs,
        check_vma=False,
    )
```

```python
import jax
import jax.numpy as jnp
from jax import lax
from jax.experimental import pallas as pl
from jax.experimental.pallas import tpu as pltpu
from jax.sharding import PartitionSpec as P

EPS = 1e-05
F32 = jnp.float32
BF16 = jnp.bfloat16
PAD = 128


def rotate(block, shift):
    count = lax.axis_size("dp")
    return lax.ppermute(block, "dp", [(i, (i + shift) % count) for i in range(count)])


def gather_units(block):
    count = lax.axis_size("dp")
    return jnp.concatenate([block] + [rotate(block, -k) for k in range(1, count)], axis=-1)


def scatter_units(total):
    count = lax.axis_size("dp")
    width = total.shape[-1] // count
    parts = total.astype(BF16)
    kept = total[..., :width].astype(F32)
    for k in range(1, count):
        kept = kept + rotate(parts[..., k * width : (k + 1) * width], k).astype(F32)
    return kept


def swap_section(block):
    return lax.ppermute(block, "section", [(0, 1), (1, 0)])


def swap_core(block):
    return lax.ppermute(block, "mp", [(i, i ^ 1) for i in range(4)])


def swap_chip(block):
    return lax.ppermute(block, "mp", [(i, i ^ 2) for i in range(4)])


def swap_both(block):
    return lax.ppermute(block, ("section", "mp"), [(i, i ^ 6) for i in range(8)])


def after(array, *others):
    return lax.optimization_barrier((array,) + others)[0]


CORE, CHIP, SECTION, OWN, PLAN = 0, 1, 2, 3, 5
STEPS = 4
VMEM_BYTES = 48 * 1024 * 1024


def step_place():
    step = pl.program_id(0)
    return step, 1 - step // 2, step % 2


def slot_at(place, a, b):
    return 2 * (place[CHIP] ^ a) + (place[CORE] ^ b)


def join_units(step, which, parts, whole):
    held, above, below, *far = parts

    @pl.when(step == 0)
    def _():
        width = held.shape[-1]
        for k, part in enumerate((held.at[which], above.at[which], far[which], below.at[which])):
            whole[:, k * width : (k + 1) * width] = part[...]


def join_slots(step, parts, whole):
    @pl.when(step == 0)
    def _():
        whole[0] = parts[0][...]
        whole[1] = parts[1][...]


def load_set(place, refs, rows):
    step, b, which = step_place()
    tokens = refs[0].shape[1]
    for k in range(2):

        @pl.when(which == k)
        def _(k=k):
            for a in range(2):
                rows[a * tokens : (a + 1) * tokens] = refs[k][slot_at(place, a, b)]


def load_top(phase, place, top, rows):
    step, b, which = step_place()
    tokens, half = top.shape[1], top.shape[0] // 2
    for a in range(2):
        slot = half * (place[OWN + phase] ^ which) + slot_at(place, a, b)
        rows[a * tokens : (a + 1) * tokens] = top[place[PLAN + slot]]


def put_partial(value, sent, kept, step, which):
    value = value.astype(BF16).reshape(sent.shape[1:])

    @pl.when(step < 2)
    def _():
        sent[which] = value

    @pl.when(step >= 2)
    def _():
        kept[which] = value


def hidden_kernel(group, place, own, received, gain, w0, w1, w2, w3, w4, sent, kept, weights, rows):
    step, b, which = step_place()
    join_units(step, 0, (w0, w1, w2, w3, w4), weights)
    load_set(place, (own, received), rows)
    wide = rows[...].astype(F32)
    normed = (wide * gain[group : group + 1, :]).astype(BF16)
    part = jnp.dot(normed, weights[...], preferred_element_type=F32)
    squares = jnp.sum(wide * wide, axis=1, keepdims=True)
    packed = jnp.concatenate((part, jnp.broadcast_to(squares, (part.shape[0], PAD))), axis=1)
    put_partial(packed, sent, kept, step, which)


def first_part_kernel(
    group, place, own, received, gain, top, w0, w1, w2, w3, w4, sent0, kept0, sent1, kept1,
    weights, outward, rows,
):
    step, b, which = step_place()
    join_units(step, 0, (w0, w1, w2, w3, w4), weights)
    join_units(step, 1, (w0, w1, w2, w3, w4), outward)
    load_set(place, (own, received), rows)
    wide = rows[...].astype(F32)
    normed = (wide * gain[group : group + 1, :]).astype(BF16)
    part = jnp.dot(normed, weights[...], preferred_element_type=F32)
    squares = jnp.sum(wide * wide, axis=1, keepdims=True)
    packed = jnp.concatenate((part, jnp.broadcast_to(squares, (part.shape[0], PAD))), axis=1)
    put_partial(packed, sent0, kept0, step, which)
    load_top(0, place, top, rows)
    part = jnp.dot(rows[...], outward[...], preferred_element_type=F32)
    put_partial(part, sent1, kept1, step, which)


def back_step(group, place, own, received, gain, spread, weights, rows, incoming):
    step, b, which = step_place()
    load_set(place, (own, received), rows)
    units = weights.shape[1]
    packed = spread[b, which].reshape(rows.shape[0], units + PAD)
    back = lax.dot_general(
        packed[:, :units], weights[...], (((1,), (1,)), ((), ())), preferred_element_type=F32
    )
    factor = packed[:, units : units + 1].astype(F32)
    result = (
        incoming.astype(F32)
        + gain[group : group + 1, :] * back
        - factor * rows[...].astype(F32)
    )
    return result.astype(BF16)


def put_result(place, result, results):
    step, b, which = step_place()
    tokens = result.shape[0] // 2
    for k in range(2):

        @pl.when(which == k)
        def _(k=k):
            for a in range(2):
                results[k][slot_at(place, a, b)] = result[a * tokens : (a + 1) * tokens]


def first_back_kernel(
    group, place, own, received, gain, top, p0, p1, w0, w1, w2, w3, w4, v0, v1, v2, v3, v4,
    result0, result1, sent, kept, weights, outward, spread, rows, grads,
):
    step, b, which = step_place()
    join_units(step, 0, (w0, w1, w2, w3, w4), weights)
    join_units(step, 1, (v0, v1, v2, v3, v4), outward)
    join_slots(step, (p0, p1), spread)
    load_top(0, place, top, grads)
    result = back_step(group, place, own, received, gain, spread, weights, rows, grads[...])
    put_result(place, result, (result0, result1))
    part = jnp.dot(result, outward[...], preferred_element_type=F32)
    put_partial(part, sent, kept, step, 1 - which)


def last_back_kernel(
    group, place, own, received, gain, in0, in1, p0, p1, w0, w1, w2, w3, w4,
    result0, result1, weights, spread, rows, grads,
):
    step, b, which = step_place()
    join_units(step, 0, (w0, w1, w2, w3, w4), weights)
    join_slots(step, (p0, p1), spread)
    load_set(place, (in0, in1), grads)
    result = back_step(group, place, own, received, gain, spread, weights, rows, grads[...])
    put_result(place, result, (result0, result1))


def add_grad(step, total, units, rows):
    part = lax.dot_general(units, rows, (((0,), (0,)), ((), ())), preferred_element_type=F32)

    @pl.when(step == 0)
    def _():
        total[...] = part

    @pl.when(step > 0)
    def _():
        total[...] += part


def put_grad(step, total, kept, parts):
    @pl.when(step == STEPS - 1)
    def _():
        height = kept.shape[0]
        kept[...] = total[:height]
        for k, part in enumerate(parts):
            part[...] = total[(k + 1) * height : (k + 2) * height].astype(BF16)


def in_grad_kernel(
    group, place, own, received, gain, p0, p1, kept, c1, c2, c3, total, spread, rows
):
    step, b, which = step_place()
    join_slots(step, (p0, p1), spread)
    load_set(place, (own, received), rows)
    normed = (rows[...].astype(F32) * gain[group : group + 1, :]).astype(BF16)
    packed = spread[b, which].reshape(rows.shape[0], spread.shape[-1])
    add_grad(step, total, packed[:, : total.shape[0]], normed)
    put_grad(step, total, kept, (c1, c2, c3))


def top_grad_kernel(place, top, p0, p1, kept, c1, c2, c3, total, spread, rows):
    step, b, which = step_place()
    join_slots(step, (p0, p1), spread)
    load_top(0, place, top, rows)
    packed = spread[b, which].reshape(rows.shape[0], spread.shape[-1])
    add_grad(step, total, packed, rows[...])
    put_grad(step, total, kept, (c1, c2, c3))


def out_grad_kernel(place, in0, in1, p0, p1, kept, c1, c2, c3, total, spread, rows):
    step, b, which = step_place()
    join_slots(step, (p0, p1), spread)
    load_set(place, (in0, in1), rows)
    packed = spread[b, which].reshape(rows.shape[0], spread.shape[-1])
    add_grad(step, total, packed, rows[...])
    put_grad(step, total, kept, (c1, c2, c3))


def core_sum_kernel(count, *refs):
    kept, moved, riders = refs[:count], refs[count : 2 * count], refs[2 * count : -4]
    own, chip, section, both = refs[-4:]
    start = 0
    for left, right in zip(kept, moved):
        width = left.shape[-1]
        for k, out in enumerate((own, chip, section, both)):
            value = left[k // 2, k % 2].astype(F32) + right[k // 2, k % 2].astype(F32)
            out[:, start : start + width] = value.astype(out.dtype)
        start += width
    for rider in riders:
        for out in (chip, section, both):
            out[:, start:] = rider[...]


def hop_sum_kernel(next_part, last_part, hop0, hop1, forth, back):
    cut = hop0.shape[0]

    def added(a, b):
        return (a.astype(F32) + b.astype(F32)).astype(BF16)

    forth[:cut] = added(next_part[:cut], hop0[...])
    forth[cut:] = next_part[cut:]
    back[:cut] = last_part[:cut]
    back[cut:] = added(last_part[cut:], hop1[...])


def whole_sum(own, parts):
    width = own.shape[1]
    total = own[...]
    for part in parts:
        total = total + part[:, :width].astype(F32)
    return total


def put_riders(four, rider, parts):
    width = rider.shape[1]
    four[0, 0] = rider[...]
    for k, part in enumerate(parts):
        four[(k + 1) // 2, (k + 1) % 2] = part[:, part.shape[1] - width :]


def put_units(features, hidden, unit_grads, packed):
    units = unit_grads.shape[1]
    unit_sums, square_sums = hidden[:, :units], hidden[:, units : units + 1]
    inverse_rms, hidden_pre, sigma, activated = row_terms(unit_sums, square_sums, features)
    scaled_grad, factor = unit_terms(
        unit_grads, unit_sums, inverse_rms, hidden_pre, sigma, features
    )
    packed[:, :units] = scaled_grad
    packed[:, units:] = jnp.broadcast_to(factor, (factor.shape[0], PAD)).astype(BF16)
    return activated


def first_unit_kernel(features, own, chip, section, both, packed, activated):
    units = activated.shape[1]
    total = whole_sum(own, (chip, section, both))
    activated[...] = put_units(features, total, total[:, units + PAD :], packed)


def active_kernel(features, own, chip, section, both, rider, hidden, activated, four):
    parts = (chip, section, both)
    total = whole_sum(own, parts)
    hidden[...] = total
    units = activated.shape[1]
    terms = row_terms(total[:, :units], total[:, units : units + 1], features)
    activated[...] = terms[3]
    put_riders(four, rider, parts)


def unit_kernel(features, hidden, own, chip, section, both, rider, packed, four):
    parts = (chip, section, both)
    put_units(features, hidden, whole_sum(own, parts), packed)
    put_riders(four, rider, parts)


def call(kernel, name, outs, args, scratch=(), specs=None, place=None, flops=0):
    size = sum(a.size * a.dtype.itemsize for a in args)
    size += sum(o.size * o.dtype.itemsize for o in outs)
    cost = pl.CostEstimate(flops=flops, bytes_accessed=size, transcendentals=0)
    params = pltpu.CompilerParams(vmem_limit_bytes=VMEM_BYTES)
    if place is None:
        return pl.pallas_call(
            kernel, out_shape=outs, compiler_params=params, cost_estimate=cost, name=name
        )(*args)

    def whole(shape):
        return pl.BlockSpec(shape, lambda i, s: (0,) * len(shape))

    specs = specs or {}
    return pl.pallas_call(
        kernel,
        out_shape=outs,
        grid_spec=pltpu.PrefetchScalarGridSpec(
            num_scalar_prefetch=1,
            grid=(STEPS,),
            in_specs=[specs.get(k, whole(a.shape)) for k, a in enumerate(args)],
            out_specs=[whole(o.shape) for o in outs],
            scratch_shapes=[pltpu.VMEM(shape, dtype) for shape, dtype in scratch],
        ),
        compiler_params=params,
        cost_estimate=cost,
        name=name,
    )(place, *args)


def shape_of(shape, dtype=BF16):
    return jax.ShapeDtypeStruct(shape, dtype)


def swap_chips(chip, section, both):
    return swap_chip(chip), swap_section(section), swap_both(both)


def core_sum(sent, kept, *riders):
    tokens = sent[0].shape[2]
    width = sum(part.shape[3] for part in sent)
    wide = width + sum(rider.shape[1] for rider in riders)

    def bound(*refs):
        core_sum_kernel(len(sent), *refs)

    return call(
        bound,
        "core_sum",
        [shape_of((tokens, width), F32)] + [shape_of((tokens, wide))] * 3,
        tuple(kept) + tuple(swap_core(part) for part in sent) + riders,
    )


def pair_spread(block):
    parts = (block,) + swap_chips(block, block, block)
    four = jnp.stack(parts).reshape((2, 2) + block.shape)
    return four, swap_core(four)


def two_sections(saved_inputs, cotangent, weight_in, weight_out, gain, plan):
    own = lax.axis_index("section")
    other = 1 - own
    mp_index = lax.axis_index("mp")
    stored = saved_inputs[0]
    slots, tokens, width = stored.shape
    half, part = slots // 2, width // 2
    features = width * lax.axis_size("mp")
    place = jnp.concatenate(
        (jnp.stack((mp_index % 2, mp_index // 2, own, other, own)).astype(jnp.int32), plan)
    )

    def rows(array, section):
        return lax.dynamic_slice_in_dim(array, section * part, part, 0)

    mine = jnp.stack((rows(weight_in[0], own), rows(weight_out[0], own)))
    moved = swap_section(jnp.stack((rows(weight_in[0], other), rows(weight_out[0], other))))

    def sent_inputs(phase):
        first = half * place[OWN + phase]
        return lax.dynamic_slice(stored, (first, 0, other * part), (half, tokens, part))

    received = swap_section(after(jnp.stack((sent_inputs(0), sent_inputs(1))), moved))

    def near(block):
        return rotate(block, 1), rotate(block, -1)

    def far(below, above):
        return rotate(below[0], 1), rotate(above[1], -1)

    held0 = jnp.where(own == 1, mine, moved)
    held1 = jnp.where(own == 0, mine, moved)
    below, above = near(held0)
    weights0 = (held0, above, below) + far(below, above)
    below, above = near(after(held1, below, above))
    weights1 = (held1, above, below) + far(below, above)
    units = 4 * mine.shape[-1]
    rows2 = 2 * tokens
    gain_spec = pl.BlockSpec((2, part), lambda i, s: (0, s[SECTION]))
    top_spec = pl.BlockSpec((slots, tokens, part), lambda i, s: (0, 0, s[SECTION]))
    partial_shapes = [shape_of((2, 2, tokens, units))] * 2
    hidden_shapes = [shape_of((2, 2, tokens, units + PAD))] * 2
    set_shape = shape_of((half, tokens, part))
    weight_scratch = ((part, units), BF16)
    rows_scratch = ((rows2, part), BF16)
    spread_scratch = ((2, 2, 2, tokens, units + PAD), BF16)
    act_scratch = ((2, 2, 2, tokens, units), BF16)
    grad_scratch = ((units, part), F32)
    grad_shapes = [shape_of((units // 4, part), F32)] + [shape_of((units // 4, part))] * 3
    four_shape = shape_of((2, 2, tokens, units))
    one_dot = 2 * slots * tokens * part * units


    def received_spec(phase):
        return pl.BlockSpec((None, half, tokens, part), lambda i, s: (phase, 0, 0, 0))

    def own_spec(phase):
        return pl.BlockSpec(
            (half, tokens, part), lambda i, s: (s[OWN + phase], 0, s[SECTION])
        )

    def bind(kernel, *first):
        def bound(*refs):
            kernel(*first, *refs)

        return bound

    def first_hop(parts):
        cut = parts[2].shape[0] // 2
        return rotate(parts[2][:cut], 1), rotate(parts[2][cut:], -1)

    def second_hop(parts, hop, *earlier):
        kept, next_part, _, last_part = parts
        forth, back = call(
            hop_sum_kernel,
            "hop_sum",
            [shape_of(next_part.shape)] * 2,
            (after(next_part, *earlier), last_part) + hop,
        )
        return kept, rotate(forth, 1), rotate(back, -1)

    def total(parts):
        return parts[0] + parts[1].astype(F32) + parts[2].astype(F32)

    sent, kept, sent1, kept1 = call(
        bind(first_part_kernel, 1),
        "first_part",
        hidden_shapes + partial_shapes,
        (stored, received, gain, cotangent) + weights0,
        [weight_scratch, weight_scratch, rows_scratch],
        {0: own_spec(0), 1: received_spec(0), 2: gain_spec, 3: top_spec},
        place,
        2 * one_dot,
    )
    own_sum, *parts = core_sum((sent, sent1), (kept, kept1))
    scaled0, act0 = call(
        bind(first_unit_kernel, features),
        "first_units",
        [shape_of((tokens, units + PAD)), shape_of((tokens, units))],
        (own_sum,) + swap_chips(*parts),
    )
    scaled0 = pair_spread(scaled0)

    sent, kept = call(
        bind(hidden_kernel, 0),
        "hidden_part",
        hidden_shapes,
        (stored, received, gain) + weights1,
        [weight_scratch, rows_scratch],
        {0: own_spec(1), 1: received_spec(1), 2: gain_spec},
        place,
        one_dot,
    )
    own_sum, *parts = core_sum((sent,), (kept,), act0)
    in_grads0 = call(
        bind(in_grad_kernel, 1),
        "in_grad",
        grad_shapes,
        (stored, received, after(gain, own_sum)) + scaled0,
        [grad_scratch, spread_scratch, rows_scratch],
        {0: own_spec(0), 1: received_spec(0), 2: gain_spec},
        place,
        one_dot,
    )
    in_hop0 = first_hop(in_grads0)
    result0, result1, sent, kept = call(
        bind(first_back_kernel, 1),
        "first_back",
        [set_shape, set_shape] + partial_shapes,
        (stored, received, after(gain, in_grads0[0]), cotangent) + scaled0 + weights0 + weights1,
        [weight_scratch, weight_scratch, spread_scratch, rows_scratch, rows_scratch],
        {0: own_spec(0), 1: received_spec(0), 2: gain_spec, 3: top_spec},
        place,
        2 * one_dot,
    )
    hidden1, act1, act0 = call(
        bind(active_kernel, features),
        "activated",
        [shape_of((tokens, units + PAD), F32), shape_of((tokens, units)), four_shape],
        (after(own_sum, kept),) + swap_chips(*parts) + (act0,),
    )
    own_sum, *parts = core_sum((sent,), (kept,), act1)
    in_totals0 = second_hop(in_grads0, in_hop0, own_sum)
    out_grads0 = call(
        top_grad_kernel,
        "top_grad",
        grad_shapes,
        (cotangent, after(act0, own_sum), swap_core(act0)),
        [grad_scratch, act_scratch, rows_scratch],
        {0: top_spec},
        place,
        one_dot,
    )
    out_hop0 = first_hop(out_grads0)
    scaled1, act1 = call(
        bind(unit_kernel, features),
        "unit_grads",
        [shape_of((tokens, units + PAD)), four_shape],
        (after(hidden1, out_grads0[0]), own_sum) + swap_chips(*parts) + (act1,),
    )
    out_totals0 = second_hop(out_grads0, out_hop0, scaled1)
    scaled1 = pair_spread(scaled1)
    out_grads1 = call(
        out_grad_kernel,
        "out_grad",
        grad_shapes,
        (result1, result0, act1, swap_core(act1)),
        [grad_scratch, act_scratch, rows_scratch],
        None,
        place,
        one_dot,
    )
    out_hop1 = first_hop(out_grads1)
    returned0 = swap_section(after(result1, scaled1[0]))
    in_grads1 = call(
        bind(in_grad_kernel, 0),
        "in_grad",
        grad_shapes,
        (stored, received, after(gain, out_grads1[0])) + scaled1,
        [grad_scratch, spread_scratch, rows_scratch],
        {0: own_spec(1), 1: received_spec(1), 2: gain_spec},
        place,
        one_dot,
    )
    in_hop1 = first_hop(in_grads1)
    result2, result3 = call(
        bind(last_back_kernel, 0),
        "last_back",
        [set_shape, set_shape],
        (stored, received, gain, result1, after(result0, in_grads1[0])) + scaled1 + weights1,
        [weight_scratch, spread_scratch, rows_scratch, rows_scratch],
        {0: own_spec(1), 1: received_spec(1), 2: gain_spec},
        place,
        one_dot,
    )
    returned1 = swap_section(result3)
    in_totals1 = second_hop(in_grads1, in_hop1, result3)
    out_totals1 = second_hop(out_grads1, out_hop1, in_grads1[0])
    in_total0, out_total0, out_total1 = total(in_totals0), total(out_totals0), total(out_totals1)
    in_total1 = total(in_totals1)
    outputs = jnp.zeros_like(stored)
    for phase, block, back in ((0, result0, returned0), (1, result2, returned1)):
        first = half * place[OWN + phase]
        outputs = lax.dynamic_update_slice(outputs, block, (first, 0, own * part))
        outputs = lax.dynamic_update_slice(outputs, back, (first, 0, other * part))

    def whole(total0, total1):
        kept = jnp.where(own == 1, total0, total1)
        given = jnp.where(own == 1, total1, total0).astype(BF16)
        back = swap_section(given).astype(F32)
        return jnp.where(
            own == 1,
            jnp.concatenate((back, kept), 1),
            jnp.concatenate((kept, back), 1),
        ).T

    return (whole(in_total0, in_total1)[None], whole(out_total0, out_total1)[None], outputs[None])


def pick(array, index, axis):
    return lax.dynamic_index_in_dim(array, index, axis, keepdims=False)


def any_sum(partial):
    sets, slots, tokens, width = partial.shape
    count = lax.axis_size("section") * lax.axis_size("mp")
    rows = partial.astype(BF16).reshape(count, sets * slots * tokens // count, width)
    moved = lax.all_to_all(rows, ("section", "mp"), 0, 0)
    return jnp.sum(moved.astype(F32), axis=0)


def any_spread(block, sets, slots, tokens):
    whole = lax.all_gather(block, ("section", "mp"), axis=0, tiled=True)
    return whole.reshape(sets, slots, tokens, block.shape[-1])


def row_terms(unit_sums, square_sums, features):
    inverse_rms = lax.rsqrt(square_sums / features + EPS)
    hidden_pre = inverse_rms * unit_sums
    sigma = jax.nn.sigmoid(hidden_pre)
    activated = (hidden_pre * sigma).astype(BF16)
    return inverse_rms, hidden_pre, sigma, activated


def unit_terms(unit_grads, unit_sums, inverse_rms, hidden_pre, sigma, features):
    grad_hidden = unit_grads * sigma * (1.0 + hidden_pre * (1.0 - sigma))
    scaled_grad = (inverse_rms * grad_hidden).astype(BF16)
    rms_term = jnp.sum(grad_hidden * unit_sums, axis=-1, keepdims=True)
    factor = inverse_rms**3 / features * rms_term
    return scaled_grad, factor


def project(rows, weights):
    return jnp.einsum("jktd,de->jkte", rows, weights, preferred_element_type=F32)


def accumulate(rows, units):
    return jnp.einsum("jktd,jkte->de", rows, units, preferred_element_type=F32)


def run_phase(stored, incoming, in_full, out_full, gain_row, features, sum_units, spread_units):
    units = in_full.shape[-1]
    wide = stored.astype(F32)
    normed = (wide * gain_row).astype(BF16)
    squares = jnp.sum(wide * wide, axis=-1, keepdims=True)
    part = project(normed, in_full)
    packed = jnp.concatenate((part, jnp.broadcast_to(squares, part.shape[:-1] + (PAD,))), axis=-1)
    hidden = sum_units(packed)
    unit_sums, square_sums = hidden[:, :units], hidden[:, units : units + 1]
    inverse_rms, hidden_pre, sigma, activated = row_terms(unit_sums, square_sums, features)
    activated = spread_units(activated)
    unit_grads = sum_units(project(incoming, out_full))
    scaled_grad, factor = unit_terms(
        unit_grads, unit_sums, inverse_rms, hidden_pre, sigma, features
    )
    factor = jnp.broadcast_to(factor.astype(BF16), (factor.shape[0], PAD))
    spread = spread_units(jnp.concatenate((scaled_grad, factor), axis=-1))
    scaled_grad, factor = spread[..., :units], spread[..., units : units + 1].astype(F32)
    back = jnp.einsum("jkte,de->jktd", scaled_grad, in_full, preferred_element_type=F32)
    result = (incoming.astype(F32) + gain_row * back - factor * wide).astype(BF16)
    return result, accumulate(normed, scaled_grad), accumulate(incoming, activated)


def any_sections(saved_inputs, cotangent, weight_in, weight_out, gain, plan):
    count = lax.axis_size("section")
    own = lax.axis_index("section")
    stored = saved_inputs[0]
    slots, tokens, width = stored.shape
    half, part = slots // 2, width // count
    features = width * lax.axis_size("mp")
    units = weight_in.shape[-1]

    def split_columns(array):
        return jnp.moveaxis(array.reshape(array.shape[:-1] + (count, part)), -2, 0)

    def moved(array):
        return lax.all_to_all(array, "section", 0, 0)

    inputs = moved(split_columns(stored))
    ins = moved(weight_in[0].reshape(count, part, units))
    outs = moved(weight_out[0].reshape(count, part, units))
    gains = pick(split_columns(gain), own, 0)
    top = lax.dynamic_slice_in_dim(cotangent, own * part, part, 2)
    incoming = jnp.stack([pick(top, plan[i], 0) for i in range(slots)])
    incoming = incoming.reshape(2, half, tokens, part)
    results = [[None, None] for _ in range(count)]
    in_blocks = [None] * count
    out_blocks = [None] * count
    for phase in range(count):
        group = count - 1 - phase
        result, in_total, out_total = run_phase(
            jnp.stack((inputs[group, :half], inputs[phase, half:])),
            incoming,
            gather_units(ins[group]),
            gather_units(outs[group]),
            gains[group],
            features,
            any_sum,
            lambda block: any_spread(block, 2, half, tokens),
        )
        in_blocks[group] = scatter_units(in_total)
        out_blocks[group] = scatter_units(out_total)
        results[group][0] = result[0]
        results[phase][1] = result[1]
        incoming = result

    def whole(blocks):
        return moved(jnp.stack(blocks).astype(BF16)).astype(F32).reshape(width, units)

    outputs = moved(jnp.stack([jnp.concatenate(pair) for pair in results]))
    outputs = jnp.moveaxis(outputs, 0, -2).reshape(stored.shape)
    return (whole(in_blocks)[None], whole(out_blocks)[None], outputs[None])


def solution(mesh):
    in_specs = (
        P("section", None, "dp", "mp"),
        P(None, "dp", "mp"),
        P("section", "mp", "dp"),
        P("section", "mp", "dp"),
        P(None, "mp"),
        P(),
    )
    out_specs = (P("section", "mp", "dp"), P("section", "mp", "dp"), P("section", None, "dp", "mp"))
    paired = mesh.shape["section"] == 2 and mesh.shape["mp"] == 4
    return jax.shard_map(
        two_sections if paired else any_sections,
        mesh=mesh,
        in_specs=in_specs,
        out_specs=out_specs,
        check_vma=False,
    )
```

```python
import jax
import jax.numpy as jnp
from jax import lax
from jax.experimental import pallas as pl
from jax.experimental.pallas import tpu as pltpu
from jax.sharding import PartitionSpec as P

EPS = 1e-05
F32 = jnp.float32
BF16 = jnp.bfloat16
PAD = 128


def rotate(block, shift):
    count = lax.axis_size("dp")
    return lax.ppermute(block, "dp", [(i, (i + shift) % count) for i in range(count)])


def gather_units(block):
    count = lax.axis_size("dp")
    return jnp.concatenate([block] + [rotate(block, -k) for k in range(1, count)], axis=-1)


def scatter_units(total):
    count = lax.axis_size("dp")
    width = total.shape[-1] // count
    parts = total.astype(BF16)
    kept = total[..., :width].astype(F32)
    for k in range(1, count):
        kept = kept + rotate(parts[..., k * width : (k + 1) * width], k).astype(F32)
    return kept


def swap_section(block):
    return lax.ppermute(block, "section", [(0, 1), (1, 0)])


def swap_core(block):
    return lax.ppermute(block, "mp", [(i, i ^ 1) for i in range(4)])


def swap_chip(block):
    return lax.ppermute(block, "mp", [(i, i ^ 2) for i in range(4)])


def swap_both(block):
    return lax.ppermute(block, ("section", "mp"), [(i, i ^ 6) for i in range(8)])


def after(array, *others):
    return lax.optimization_barrier((array,) + others)[0]


CORE, CHIP, SECTION, OWN, PLAN = 0, 1, 2, 3, 5
STEPS = 4
VMEM_BYTES = 48 * 1024 * 1024


def step_place():
    step = pl.program_id(0)
    return step, 1 - step // 2, step % 2


def slot_at(place, a, b):
    return 2 * (place[CHIP] ^ a) + (place[CORE] ^ b)


def join_units(step, which, parts, whole):
    held, above, below, *far = parts

    @pl.when(step == 0)
    def _():
        width = held.shape[-1]
        for k, part in enumerate((held.at[which], above.at[which], far[which], below.at[which])):
            whole[:, k * width : (k + 1) * width] = part[...]


def join_slots(step, parts, whole):
    @pl.when(step == 0)
    def _():
        whole[0] = parts[0][...]
        whole[1] = parts[1][...]


def load_set(place, refs, rows):
    step, b, which = step_place()
    tokens = refs[0].shape[1]
    for k in range(2):

        @pl.when(which == k)
        def _(k=k):
            for a in range(2):
                rows[a * tokens : (a + 1) * tokens] = refs[k][slot_at(place, a, b)]


def load_top(phase, place, top, rows):
    step, b, which = step_place()
    tokens, half = top.shape[1], top.shape[0] // 2
    for a in range(2):
        slot = half * (place[OWN + phase] ^ which) + slot_at(place, a, b)
        rows[a * tokens : (a + 1) * tokens] = top[place[PLAN + slot]]


def put_partial(value, sent, kept, step, which):
    value = value.astype(BF16).reshape(sent.shape[1:])

    @pl.when(step < 2)
    def _():
        sent[which] = value

    @pl.when(step >= 2)
    def _():
        kept[which] = value


def hidden_kernel(group, place, own, received, gain, w0, w1, w2, w3, w4, sent, kept, weights, rows):
    step, b, which = step_place()
    join_units(step, 0, (w0, w1, w2, w3, w4), weights)
    load_set(place, (own, received), rows)
    wide = rows[...].astype(F32)
    normed = (wide * gain[group : group + 1, :]).astype(BF16)
    part = jnp.dot(normed, weights[...], preferred_element_type=F32)
    squares = jnp.sum(wide * wide, axis=1, keepdims=True)
    packed = jnp.concatenate((part, jnp.broadcast_to(squares, (part.shape[0], PAD))), axis=1)
    put_partial(packed, sent, kept, step, which)


def first_part_kernel(
    group, place, own, received, gain, top, w0, w1, w2, w3, w4, sent0, kept0, sent1, kept1,
    weights, outward, rows,
):
    step, b, which = step_place()
    join_units(step, 0, (w0, w1, w2, w3, w4), weights)
    join_units(step, 1, (w0, w1, w2, w3, w4), outward)
    load_set(place, (own, received), rows)
    wide = rows[...].astype(F32)
    normed = (wide * gain[group : group + 1, :]).astype(BF16)
    part = jnp.dot(normed, weights[...], preferred_element_type=F32)
    squares = jnp.sum(wide * wide, axis=1, keepdims=True)
    packed = jnp.concatenate((part, jnp.broadcast_to(squares, (part.shape[0], PAD))), axis=1)
    put_partial(packed, sent0, kept0, step, which)
    load_top(0, place, top, rows)
    part = jnp.dot(rows[...], outward[...], preferred_element_type=F32)
    put_partial(part, sent1, kept1, step, which)


def back_step(group, place, own, received, gain, spread, weights, rows, incoming):
    step, b, which = step_place()
    load_set(place, (own, received), rows)
    units = weights.shape[1]
    packed = spread[b, which].reshape(rows.shape[0], units + PAD)
    back = lax.dot_general(
        packed[:, :units], weights[...], (((1,), (1,)), ((), ())), preferred_element_type=F32
    )
    factor = packed[:, units : units + 1].astype(F32)
    result = (
        incoming.astype(F32)
        + gain[group : group + 1, :] * back
        - factor * rows[...].astype(F32)
    )
    return result.astype(BF16)


def put_result(place, result, results):
    step, b, which = step_place()
    tokens = result.shape[0] // 2
    for k in range(2):

        @pl.when(which == k)
        def _(k=k):
            for a in range(2):
                results[k][slot_at(place, a, b)] = result[a * tokens : (a + 1) * tokens]


def first_back_kernel(
    group, place, own, received, gain, top, p0, p1, w0, w1, w2, w3, w4, v0, v1, v2, v3, v4,
    result0, result1, sent, kept, weights, outward, spread, rows, grads,
):
    step, b, which = step_place()
    join_units(step, 0, (w0, w1, w2, w3, w4), weights)
    join_units(step, 1, (v0, v1, v2, v3, v4), outward)
    join_slots(step, (p0, p1), spread)
    load_top(0, place, top, grads)
    result = back_step(group, place, own, received, gain, spread, weights, rows, grads[...])
    put_result(place, result, (result0, result1))
    part = jnp.dot(result, outward[...], preferred_element_type=F32)
    put_partial(part, sent, kept, step, 1 - which)


def last_back_kernel(
    group, place, own, received, gain, in0, in1, p0, p1, w0, w1, w2, w3, w4,
    result0, result1, weights, spread, rows, grads,
):
    step, b, which = step_place()
    join_units(step, 0, (w0, w1, w2, w3, w4), weights)
    join_slots(step, (p0, p1), spread)
    load_set(place, (in0, in1), grads)
    result = back_step(group, place, own, received, gain, spread, weights, rows, grads[...])
    put_result(place, result, (result0, result1))


def add_grad(step, total, units, rows):
    part = lax.dot_general(units, rows, (((0,), (0,)), ((), ())), preferred_element_type=F32)

    @pl.when(step == 0)
    def _():
        total[...] = part

    @pl.when(step > 0)
    def _():
        total[...] += part


def put_grad(step, total, kept, parts):
    @pl.when(step == STEPS - 1)
    def _():
        height = kept.shape[0]
        kept[...] = total[:height]
        for k, part in enumerate(parts):
            part[...] = total[(k + 1) * height : (k + 2) * height].astype(BF16)


def in_grad_kernel(
    group, place, own, received, gain, p0, p1, kept, c1, c2, c3, total, spread, rows
):
    step, b, which = step_place()
    join_slots(step, (p0, p1), spread)
    load_set(place, (own, received), rows)
    normed = (rows[...].astype(F32) * gain[group : group + 1, :]).astype(BF16)
    packed = spread[b, which].reshape(rows.shape[0], spread.shape[-1])
    add_grad(step, total, packed[:, : total.shape[0]], normed)
    put_grad(step, total, kept, (c1, c2, c3))


def top_grad_kernel(place, top, p0, p1, kept, c1, c2, c3, total, spread, rows):
    step, b, which = step_place()
    join_slots(step, (p0, p1), spread)
    load_top(0, place, top, rows)
    packed = spread[b, which].reshape(rows.shape[0], spread.shape[-1])
    add_grad(step, total, packed, rows[...])
    put_grad(step, total, kept, (c1, c2, c3))


def out_grad_kernel(place, in0, in1, p0, p1, kept, c1, c2, c3, total, spread, rows):
    step, b, which = step_place()
    join_slots(step, (p0, p1), spread)
    load_set(place, (in0, in1), rows)
    packed = spread[b, which].reshape(rows.shape[0], spread.shape[-1])
    add_grad(step, total, packed, rows[...])
    put_grad(step, total, kept, (c1, c2, c3))


def core_sum_kernel(count, *refs):
    kept, moved, riders = refs[:count], refs[count : 2 * count], refs[2 * count : -4]
    own, chip, section, both = refs[-4:]
    start = 0
    for left, right in zip(kept, moved):
        width = left.shape[-1]
        for k, out in enumerate((own, chip, section, both)):
            value = left[k // 2, k % 2].astype(F32) + right[k // 2, k % 2].astype(F32)
            out[:, start : start + width] = value.astype(out.dtype)
        start += width
    for rider in riders:
        for out in (chip, section, both):
            out[:, start:] = rider[...]


def hop_sum_kernel(next_part, last_part, hop0, hop1, forth, back):
    cut = hop0.shape[0]

    def added(a, b):
        return (a.astype(F32) + b.astype(F32)).astype(BF16)

    forth[:cut] = added(next_part[:cut], hop0[...])
    forth[cut:] = next_part[cut:]
    back[:cut] = last_part[:cut]
    back[cut:] = added(last_part[cut:], hop1[...])


def whole_sum(own, parts):
    width = own.shape[1]
    total = own[...]
    for part in parts:
        total = total + part[:, :width].astype(F32)
    return total


def put_riders(four, rider, parts):
    width = rider.shape[1]
    four[0, 0] = rider[...]
    for k, part in enumerate(parts):
        four[(k + 1) // 2, (k + 1) % 2] = part[:, part.shape[1] - width :]


def put_units(features, hidden, unit_grads, packed):
    units = unit_grads.shape[1]
    unit_sums, square_sums = hidden[:, :units], hidden[:, units : units + 1]
    inverse_rms, hidden_pre, sigma, activated = row_terms(unit_sums, square_sums, features)
    scaled_grad, factor = unit_terms(
        unit_grads, unit_sums, inverse_rms, hidden_pre, sigma, features
    )
    packed[:, :units] = scaled_grad
    packed[:, units:] = jnp.broadcast_to(factor, (factor.shape[0], PAD)).astype(BF16)
    return activated


def first_unit_kernel(features, own, chip, section, both, packed, activated):
    units = activated.shape[1]
    total = whole_sum(own, (chip, section, both))
    activated[...] = put_units(features, total, total[:, units + PAD :], packed)


def active_kernel(features, own, chip, section, both, rider, hidden, activated, four):
    parts = (chip, section, both)
    total = whole_sum(own, parts)
    hidden[...] = total
    units = activated.shape[1]
    terms = row_terms(total[:, :units], total[:, units : units + 1], features)
    activated[...] = terms[3]
    put_riders(four, rider, parts)


def unit_kernel(features, hidden, own, chip, section, both, rider, packed, four):
    parts = (chip, section, both)
    put_units(features, hidden, whole_sum(own, parts), packed)
    put_riders(four, rider, parts)


def call(kernel, name, outs, args, scratch=(), specs=None, place=None, flops=0):
    size = sum(a.size * a.dtype.itemsize for a in args)
    size += sum(o.size * o.dtype.itemsize for o in outs)
    cost = pl.CostEstimate(flops=flops, bytes_accessed=size, transcendentals=0)
    params = pltpu.CompilerParams(vmem_limit_bytes=VMEM_BYTES)
    if place is None:
        return pl.pallas_call(
            kernel, out_shape=outs, compiler_params=params, cost_estimate=cost, name=name
        )(*args)

    def whole(shape):
        return pl.BlockSpec(shape, lambda i, s: (0,) * len(shape))

    specs = specs or {}
    return pl.pallas_call(
        kernel,
        out_shape=outs,
        grid_spec=pltpu.PrefetchScalarGridSpec(
            num_scalar_prefetch=1,
            grid=(STEPS,),
            in_specs=[specs.get(k, whole(a.shape)) for k, a in enumerate(args)],
            out_specs=[whole(o.shape) for o in outs],
            scratch_shapes=[pltpu.VMEM(shape, dtype) for shape, dtype in scratch],
        ),
        compiler_params=params,
        cost_estimate=cost,
        name=name,
    )(place, *args)


def shape_of(shape, dtype=BF16):
    return jax.ShapeDtypeStruct(shape, dtype)


def swap_chips(chip, section, both):
    return swap_chip(chip), swap_section(section), swap_both(both)


def core_sum(sent, kept, *riders):
    tokens = sent[0].shape[2]
    width = sum(part.shape[3] for part in sent)
    wide = width + sum(rider.shape[1] for rider in riders)

    def bound(*refs):
        core_sum_kernel(len(sent), *refs)

    return call(
        bound,
        "core_sum",
        [shape_of((tokens, width), F32)] + [shape_of((tokens, wide))] * 3,
        tuple(kept) + tuple(swap_core(part) for part in sent) + riders,
    )


def pair_spread(block, *earlier):
    parts = (block,) + swap_chips(block, block, block)
    four = after(jnp.stack(parts).reshape((2, 2) + block.shape), *earlier)
    return four, swap_core(four)


def two_sections(saved_inputs, cotangent, weight_in, weight_out, gain, plan):
    own = lax.axis_index("section")
    other = 1 - own
    mp_index = lax.axis_index("mp")
    stored = saved_inputs[0]
    slots, tokens, width = stored.shape
    half, part = slots // 2, width // 2
    features = width * lax.axis_size("mp")
    place = jnp.concatenate(
        (jnp.stack((mp_index % 2, mp_index // 2, own, other, own)).astype(jnp.int32), plan)
    )

    def rows(array, section):
        return lax.dynamic_slice_in_dim(array, section * part, part, 0)

    mine = jnp.stack((rows(weight_in[0], own), rows(weight_out[0], own)))
    moved = swap_section(jnp.stack((rows(weight_in[0], other), rows(weight_out[0], other))))

    def sent_inputs(phase):
        first = half * place[OWN + phase]
        return lax.dynamic_slice(stored, (first, 0, other * part), (half, tokens, part))

    received = swap_section(after(jnp.stack((sent_inputs(0), sent_inputs(1))), moved))

    def near(block):
        return rotate(block, 1), rotate(block, -1)

    def far(below, above):
        return rotate(below[0], 1), rotate(above[1], -1)

    held0 = jnp.where(own == 1, mine, moved)
    held1 = jnp.where(own == 0, mine, moved)
    below, above = near(held0)
    weights0 = (held0, above, below) + far(below, above)
    below, above = near(after(held1, below, above))
    weights1 = (held1, above, below) + far(below, above)
    units = 4 * mine.shape[-1]
    rows2 = 2 * tokens
    gain_spec = pl.BlockSpec((2, part), lambda i, s: (0, s[SECTION]))
    top_spec = pl.BlockSpec((slots, tokens, part), lambda i, s: (0, 0, s[SECTION]))
    partial_shapes = [shape_of((2, 2, tokens, units))] * 2
    hidden_shapes = [shape_of((2, 2, tokens, units + PAD))] * 2
    set_shape = shape_of((half, tokens, part))
    weight_scratch = ((part, units), BF16)
    rows_scratch = ((rows2, part), BF16)
    spread_scratch = ((2, 2, 2, tokens, units + PAD), BF16)
    act_scratch = ((2, 2, 2, tokens, units), BF16)
    grad_scratch = ((units, part), F32)
    grad_shapes = [shape_of((units // 4, part), F32)] + [shape_of((units // 4, part))] * 3
    four_shape = shape_of((2, 2, tokens, units))
    one_dot = 2 * slots * tokens * part * units


    def received_spec(phase):
        return pl.BlockSpec((None, half, tokens, part), lambda i, s: (phase, 0, 0, 0))

    def own_spec(phase):
        return pl.BlockSpec(
            (half, tokens, part), lambda i, s: (s[OWN + phase], 0, s[SECTION])
        )

    def bind(kernel, *first):
        def bound(*refs):
            kernel(*first, *refs)

        return bound

    def first_hop(parts):
        cut = parts[2].shape[0] // 2
        return rotate(parts[2][:cut], 1), rotate(parts[2][cut:], -1)

    def second_hop(parts, hop, *earlier):
        kept, next_part, _, last_part = parts
        forth, back = call(
            hop_sum_kernel,
            "hop_sum",
            [shape_of(next_part.shape)] * 2,
            (after(next_part, *earlier), last_part) + hop,
        )
        return kept, rotate(forth, 1), rotate(back, -1)

    def total(parts):
        return parts[0] + parts[1].astype(F32) + parts[2].astype(F32)

    sent, kept, sent1, kept1 = call(
        bind(first_part_kernel, 1),
        "first_part",
        hidden_shapes + partial_shapes,
        (stored, received, gain, cotangent) + weights0,
        [weight_scratch, weight_scratch, rows_scratch],
        {0: own_spec(0), 1: received_spec(0), 2: gain_spec, 3: top_spec},
        place,
        2 * one_dot,
    )
    own_sum, *parts = core_sum((sent, sent1), (kept, kept1))
    scaled0, act0 = call(
        bind(first_unit_kernel, features),
        "first_units",
        [shape_of((tokens, units + PAD)), shape_of((tokens, units))],
        (own_sum,) + swap_chips(*parts),
    )
    scaled0 = pair_spread(scaled0)

    sent, kept = call(
        bind(hidden_kernel, 0),
        "hidden_part",
        hidden_shapes,
        (stored, received, gain) + weights1,
        [weight_scratch, rows_scratch],
        {0: own_spec(1), 1: received_spec(1), 2: gain_spec},
        place,
        one_dot,
    )
    own_sum, *parts = core_sum((sent,), (kept,), act0)
    in_grads0 = call(
        bind(in_grad_kernel, 1),
        "in_grad",
        grad_shapes,
        (stored, received, after(gain, own_sum)) + scaled0,
        [grad_scratch, spread_scratch, rows_scratch],
        {0: own_spec(0), 1: received_spec(0), 2: gain_spec},
        place,
        one_dot,
    )
    in_hop0 = first_hop(in_grads0)
    result0, result1, sent, kept = call(
        bind(first_back_kernel, 1),
        "first_back",
        [set_shape, set_shape] + partial_shapes,
        (stored, received, after(gain, in_grads0[0]), cotangent) + scaled0 + weights0 + weights1,
        [weight_scratch, weight_scratch, spread_scratch, rows_scratch, rows_scratch],
        {0: own_spec(0), 1: received_spec(0), 2: gain_spec, 3: top_spec},
        place,
        2 * one_dot,
    )
    hidden1, act1, act0 = call(
        bind(active_kernel, features),
        "activated",
        [shape_of((tokens, units + PAD), F32), shape_of((tokens, units)), four_shape],
        (after(own_sum, kept),) + swap_chips(*parts) + (act0,),
    )
    own_sum, *parts = core_sum((after(sent, *in_hop0),), (kept,), act1)
    in_totals0 = second_hop(in_grads0, in_hop0, own_sum)
    out_grads0 = call(
        top_grad_kernel,
        "top_grad",
        grad_shapes,
        (cotangent, after(act0, own_sum), swap_core(act0)),
        [grad_scratch, act_scratch, rows_scratch],
        {0: top_spec},
        place,
        one_dot,
    )
    out_hop0 = first_hop(out_grads0)
    scaled1, act1 = call(
        bind(unit_kernel, features),
        "unit_grads",
        [shape_of((tokens, units + PAD)), four_shape],
        (after(hidden1, out_grads0[0], *in_totals0[1:]), own_sum) + swap_chips(*parts) + (act1,),
    )
    out_totals0 = second_hop(out_grads0, out_hop0, scaled1)
    scaled1 = pair_spread(scaled1, *out_hop0)
    out_grads1 = call(
        out_grad_kernel,
        "out_grad",
        grad_shapes,
        (result1, result0, act1, swap_core(act1)),
        [grad_scratch, act_scratch, rows_scratch],
        None,
        place,
        one_dot,
    )
    out_hop1 = first_hop(out_grads1)
    returned0 = swap_section(after(result1, scaled1[0]))
    result2, result3 = call(
        bind(last_back_kernel, 0),
        "last_back",
        [set_shape, set_shape],
        (stored, received, gain, result1, result0) + scaled1 + weights1,
        [weight_scratch, spread_scratch, rows_scratch, rows_scratch],
        {0: own_spec(1), 1: received_spec(1), 2: gain_spec},
        place,
        one_dot,
    )
    returned1 = swap_section(result3)
    in_grads1 = call(
        bind(in_grad_kernel, 0),
        "in_grad",
        grad_shapes,
        (stored, received, after(gain, out_grads1[0], result3)) + scaled1,
        [grad_scratch, spread_scratch, rows_scratch],
        {0: own_spec(1), 1: received_spec(1), 2: gain_spec},
        place,
        one_dot,
    )
    in_hop1 = first_hop(in_grads1)
    in_totals1 = second_hop(in_grads1, in_hop1, returned0)
    out_totals1 = second_hop(out_grads1, out_hop1, in_grads1[0])
    in_total0, out_total0, out_total1 = total(in_totals0), total(out_totals0), total(out_totals1)
    in_total1 = total(in_totals1)
    outputs = jnp.zeros_like(stored)
    for phase, block, back in ((0, result0, returned0), (1, result2, returned1)):
        first = half * place[OWN + phase]
        outputs = lax.dynamic_update_slice(outputs, block, (first, 0, own * part))
        outputs = lax.dynamic_update_slice(outputs, back, (first, 0, other * part))

    def whole(total0, total1):
        kept = jnp.where(own == 1, total0, total1)
        given = jnp.where(own == 1, total1, total0).astype(BF16)
        back = swap_section(given).astype(F32)
        return jnp.where(
            own == 1,
            jnp.concatenate((back, kept), 1),
            jnp.concatenate((kept, back), 1),
        ).T

    return (whole(in_total0, in_total1)[None], whole(out_total0, out_total1)[None], outputs[None])


def pick(array, index, axis):
    return lax.dynamic_index_in_dim(array, index, axis, keepdims=False)


def any_sum(partial):
    sets, slots, tokens, width = partial.shape
    count = lax.axis_size("section") * lax.axis_size("mp")
    rows = partial.astype(BF16).reshape(count, sets * slots * tokens // count, width)
    moved = lax.all_to_all(rows, ("section", "mp"), 0, 0)
    return jnp.sum(moved.astype(F32), axis=0)


def any_spread(block, sets, slots, tokens):
    whole = lax.all_gather(block, ("section", "mp"), axis=0, tiled=True)
    return whole.reshape(sets, slots, tokens, block.shape[-1])


def row_terms(unit_sums, square_sums, features):
    inverse_rms = lax.rsqrt(square_sums / features + EPS)
    hidden_pre = inverse_rms * unit_sums
    sigma = jax.nn.sigmoid(hidden_pre)
    activated = (hidden_pre * sigma).astype(BF16)
    return inverse_rms, hidden_pre, sigma, activated


def unit_terms(unit_grads, unit_sums, inverse_rms, hidden_pre, sigma, features):
    grad_hidden = unit_grads * sigma * (1.0 + hidden_pre * (1.0 - sigma))
    scaled_grad = (inverse_rms * grad_hidden).astype(BF16)
    rms_term = jnp.sum(grad_hidden * unit_sums, axis=-1, keepdims=True)
    factor = inverse_rms**3 / features * rms_term
    return scaled_grad, factor


def project(rows, weights):
    return jnp.einsum("jktd,de->jkte", rows, weights, preferred_element_type=F32)


def accumulate(rows, units):
    return jnp.einsum("jktd,jkte->de", rows, units, preferred_element_type=F32)


def run_phase(stored, incoming, in_full, out_full, gain_row, features, sum_units, spread_units):
    units = in_full.shape[-1]
    wide = stored.astype(F32)
    normed = (wide * gain_row).astype(BF16)
    squares = jnp.sum(wide * wide, axis=-1, keepdims=True)
    part = project(normed, in_full)
    packed = jnp.concatenate((part, jnp.broadcast_to(squares, part.shape[:-1] + (PAD,))), axis=-1)
    hidden = sum_units(packed)
    unit_sums, square_sums = hidden[:, :units], hidden[:, units : units + 1]
    inverse_rms, hidden_pre, sigma, activated = row_terms(unit_sums, square_sums, features)
    activated = spread_units(activated)
    unit_grads = sum_units(project(incoming, out_full))
    scaled_grad, factor = unit_terms(
        unit_grads, unit_sums, inverse_rms, hidden_pre, sigma, features
    )
    factor = jnp.broadcast_to(factor.astype(BF16), (factor.shape[0], PAD))
    spread = spread_units(jnp.concatenate((scaled_grad, factor), axis=-1))
    scaled_grad, factor = spread[..., :units], spread[..., units : units + 1].astype(F32)
    back = jnp.einsum("jkte,de->jktd", scaled_grad, in_full, preferred_element_type=F32)
    result = (incoming.astype(F32) + gain_row * back - factor * wide).astype(BF16)
    return result, accumulate(normed, scaled_grad), accumulate(incoming, activated)


def any_sections(saved_inputs, cotangent, weight_in, weight_out, gain, plan):
    count = lax.axis_size("section")
    own = lax.axis_index("section")
    stored = saved_inputs[0]
    slots, tokens, width = stored.shape
    half, part = slots // 2, width // count
    features = width * lax.axis_size("mp")
    units = weight_in.shape[-1]

    def split_columns(array):
        return jnp.moveaxis(array.reshape(array.shape[:-1] + (count, part)), -2, 0)

    def moved(array):
        return lax.all_to_all(array, "section", 0, 0)

    inputs = moved(split_columns(stored))
    ins = moved(weight_in[0].reshape(count, part, units))
    outs = moved(weight_out[0].reshape(count, part, units))
    gains = pick(split_columns(gain), own, 0)
    top = lax.dynamic_slice_in_dim(cotangent, own * part, part, 2)
    incoming = jnp.stack([pick(top, plan[i], 0) for i in range(slots)])
    incoming = incoming.reshape(2, half, tokens, part)
    results = [[None, None] for _ in range(count)]
    in_blocks = [None] * count
    out_blocks = [None] * count
    for phase in range(count):
        group = count - 1 - phase
        result, in_total, out_total = run_phase(
            jnp.stack((inputs[group, :half], inputs[phase, half:])),
            incoming,
            gather_units(ins[group]),
            gather_units(outs[group]),
            gains[group],
            features,
            any_sum,
            lambda block: any_spread(block, 2, half, tokens),
        )
        in_blocks[group] = scatter_units(in_total)
        out_blocks[group] = scatter_units(out_total)
        results[group][0] = result[0]
        results[phase][1] = result[1]
        incoming = result

    def whole(blocks):
        return moved(jnp.stack(blocks).astype(BF16)).astype(F32).reshape(width, units)

    outputs = moved(jnp.stack([jnp.concatenate(pair) for pair in results]))
    outputs = jnp.moveaxis(outputs, 0, -2).reshape(stored.shape)
    return (whole(in_blocks)[None], whole(out_blocks)[None], outputs[None])


def solution(mesh):
    in_specs = (
        P("section", None, "dp", "mp"),
        P(None, "dp", "mp"),
        P("section", "mp", "dp"),
        P("section", "mp", "dp"),
        P(None, "mp"),
        P(),
    )
    out_specs = (P("section", "mp", "dp"), P("section", "mp", "dp"), P("section", None, "dp", "mp"))
    paired = mesh.shape["section"] == 2 and mesh.shape["mp"] == 4
    return jax.shard_map(
        two_sections if paired else any_sections,
        mesh=mesh,
        in_specs=in_specs,
        out_specs=out_specs,
        check_vma=False,
    )
```

```python
import jax
import jax.numpy as jnp
from jax import lax
from jax.experimental import pallas as pl
from jax.experimental.pallas import tpu as pltpu
from jax.sharding import PartitionSpec as P

EPS = 1e-05
F32 = jnp.float32
BF16 = jnp.bfloat16
PAD = 128


def rotate(block, shift):
    count = lax.axis_size("dp")
    return lax.ppermute(block, "dp", [(i, (i + shift) % count) for i in range(count)])


def gather_units(block):
    count = lax.axis_size("dp")
    return jnp.concatenate([block] + [rotate(block, -k) for k in range(1, count)], axis=-1)


def scatter_units(total):
    count = lax.axis_size("dp")
    width = total.shape[-1] // count
    parts = total.astype(BF16)
    kept = total[..., :width].astype(F32)
    for k in range(1, count):
        kept = kept + rotate(parts[..., k * width : (k + 1) * width], k).astype(F32)
    return kept


def swap_section(block):
    return lax.ppermute(block, "section", [(0, 1), (1, 0)])


def swap_core(block):
    return lax.ppermute(block, "mp", [(i, i ^ 1) for i in range(4)])


def swap_chip(block):
    return lax.ppermute(block, "mp", [(i, i ^ 2) for i in range(4)])


def swap_both(block):
    return lax.ppermute(block, ("section", "mp"), [(i, i ^ 6) for i in range(8)])


def after(array, *others):
    return lax.optimization_barrier((array,) + others)[0]


CORE, CHIP, SECTION, OWN, PLAN = 0, 1, 2, 3, 5
STEPS = 4
VMEM_BYTES = 48 * 1024 * 1024


def step_place():
    step = pl.program_id(0)
    return step, 1 - step // 2, step % 2


def slot_at(place, a, b):
    return 2 * (place[CHIP] ^ a) + (place[CORE] ^ b)


def join_units(step, which, parts, whole):
    held, above, below, *far = parts

    @pl.when(step == 0)
    def _():
        width = held.shape[-1]
        for k, part in enumerate((held.at[which], above.at[which], far[which], below.at[which])):
            whole[:, k * width : (k + 1) * width] = part[...]


def join_whole(step, parts, whole):
    @pl.when(step == 0)
    def _():
        for k, part in enumerate(parts):
            whole[:, k * part.shape[1] : (k + 1) * part.shape[1]] = part[...]


def join_slots(step, parts, whole):
    @pl.when(step == 0)
    def _():
        whole[0] = parts[0][...]
        whole[1] = parts[1][...]


def load_set(place, refs, rows):
    step, b, which = step_place()
    tokens = refs[0].shape[1]
    for k in range(2):

        @pl.when(which == k)
        def _(k=k):
            for a in range(2):
                rows[a * tokens : (a + 1) * tokens] = refs[k][slot_at(place, a, b)]


def load_top(phase, place, top, rows):
    step, b, which = step_place()
    tokens, half = top.shape[1], top.shape[0] // 2
    for a in range(2):
        slot = half * (place[OWN + phase] ^ which) + slot_at(place, a, b)
        rows[a * tokens : (a + 1) * tokens] = top[place[PLAN + slot]]


def put_partial(value, sent, kept, step, which):
    value = value.astype(BF16).reshape(sent.shape[1:])

    @pl.when(step < 2)
    def _():
        sent[which] = value

    @pl.when(step >= 2)
    def _():
        kept[which] = value


def hidden_kernel(group, place, own, received, gain, w0, w1, w2, w3, w4, sent, kept, weights, rows):
    step, b, which = step_place()
    join_units(step, 0, (w0, w1, w2, w3, w4), weights)
    load_set(place, (own, received), rows)
    wide = rows[...].astype(F32)
    normed = (wide * gain[group : group + 1, :]).astype(BF16)
    part = jnp.dot(normed, weights[...], preferred_element_type=F32)
    squares = jnp.sum(wide * wide, axis=1, keepdims=True)
    packed = jnp.concatenate((part, jnp.broadcast_to(squares, (part.shape[0], PAD))), axis=1)
    put_partial(packed, sent, kept, step, which)


def first_part_kernel(
    group, place, own, received, gain, top, w0, w1, w2, w3, w4, w5, w6, w7, sent0, kept0, sent1, kept1,
    weights, outward, rows,
):
    step, b, which = step_place()
    join_whole(step, (w0, w1, w2, w3), weights)
    join_whole(step, (w4, w5, w6, w7), outward)
    load_set(place, (own, received), rows)
    wide = rows[...].astype(F32)
    normed = (wide * gain[group : group + 1, :]).astype(BF16)
    part = jnp.dot(normed, weights[...], preferred_element_type=F32)
    squares = jnp.sum(wide * wide, axis=1, keepdims=True)
    packed = jnp.concatenate((part, jnp.broadcast_to(squares, (part.shape[0], PAD))), axis=1)
    put_partial(packed, sent0, kept0, step, which)
    load_top(0, place, top, rows)
    part = jnp.dot(rows[...], outward[...], preferred_element_type=F32)
    put_partial(part, sent1, kept1, step, which)


def back_step(group, place, own, received, gain, spread, weights, rows, incoming):
    step, b, which = step_place()
    load_set(place, (own, received), rows)
    units = weights.shape[1]
    packed = spread[b, which].reshape(rows.shape[0], units + PAD)
    back = lax.dot_general(
        packed[:, :units], weights[...], (((1,), (1,)), ((), ())), preferred_element_type=F32
    )
    factor = packed[:, units : units + 1].astype(F32)
    result = (
        incoming.astype(F32)
        + gain[group : group + 1, :] * back
        - factor * rows[...].astype(F32)
    )
    return result.astype(BF16)


def put_result(place, result, results):
    step, b, which = step_place()
    tokens = result.shape[0] // 2
    for k in range(2):

        @pl.when(which == k)
        def _(k=k):
            for a in range(2):
                results[k][slot_at(place, a, b)] = result[a * tokens : (a + 1) * tokens]


def first_back_kernel(
    group, place, own, received, gain, top, p0, p1, w0, w1, w2, w3, v0, v1, v2, v3, v4,
    result0, result1, sent, kept, weights, outward, spread, rows, grads,
):
    step, b, which = step_place()
    join_whole(step, (w0, w1, w2, w3), weights)
    join_units(step, 1, (v0, v1, v2, v3, v4), outward)
    join_slots(step, (p0, p1), spread)
    load_top(0, place, top, grads)
    result = back_step(group, place, own, received, gain, spread, weights, rows, grads[...])
    put_result(place, result, (result0, result1))
    part = jnp.dot(result, outward[...], preferred_element_type=F32)
    put_partial(part, sent, kept, step, 1 - which)


def last_back_kernel(
    group, place, own, received, gain, in0, in1, p0, p1, w0, w1, w2, w3, w4,
    result0, result1, weights, spread, rows, grads,
):
    step, b, which = step_place()
    join_units(step, 0, (w0, w1, w2, w3, w4), weights)
    join_slots(step, (p0, p1), spread)
    load_set(place, (in0, in1), grads)
    result = back_step(group, place, own, received, gain, spread, weights, rows, grads[...])
    put_result(place, result, (result0, result1))


def flip_slots(parts, flipped):
    @pl.when(pl.program_id(0) == 0)
    def _():
        units = flipped.shape[0]
        for k in range(8):
            block = parts[k // 4][k // 2 % 2, k % 2]
            tokens = block.shape[0]
            flipped[:, k * tokens : (k + 1) * tokens] = block[:, :units].T


def fill_rows(place, load, rows):
    for k in range(8):
        block = load(k // 2 % 2, slot_at(place, k % 2, k // 4))
        tokens = block.shape[0]
        rows[k * tokens : (k + 1) * tokens] = block


def put_grad(flipped, rows, kept, parts):
    value = jnp.dot(flipped[...], rows[...], preferred_element_type=F32)
    height = kept.shape[0]
    kept[...] = value[:height]
    for k, part in enumerate(parts):
        part[...] = value[(k + 1) * height : (k + 2) * height].astype(BF16)


def in_grad_kernel(
    group, place, own, received, gain, p0, p1, kept, c1, c2, c3, flipped, rows
):
    def load(which, slot):
        block = (own, received)[which][slot].astype(F32)
        return (block * gain[group : group + 1, :]).astype(BF16)

    flip_slots((p0, p1), flipped)
    fill_rows(place, load, rows)
    put_grad(flipped, rows, kept, (c1, c2, c3))


def top_grad_kernel(place, top, p0, p1, kept, c1, c2, c3, flipped, rows):
    half = top.shape[0] // 2

    def load(which, slot):
        return top[place[PLAN + half * (place[OWN] ^ which) + slot]]

    flip_slots((p0, p1), flipped)
    fill_rows(place, load, rows)
    put_grad(flipped, rows, kept, (c1, c2, c3))


def out_grad_kernel(place, in0, in1, p0, p1, kept, c1, c2, c3, flipped, rows):
    flip_slots((p0, p1), flipped)
    fill_rows(place, lambda which, slot: (in0, in1)[which][slot], rows)
    put_grad(flipped, rows, kept, (c1, c2, c3))


def core_sum_kernel(count, *refs):
    kept, moved, riders = refs[:count], refs[count : 2 * count], refs[2 * count : -4]
    own, chip, section, both = refs[-4:]
    start = 0
    for left, right in zip(kept, moved):
        width = left.shape[-1]
        for k, out in enumerate((own, chip, section, both)):
            value = left[k // 2, k % 2].astype(F32) + right[k // 2, k % 2].astype(F32)
            out[:, start : start + width] = value.astype(out.dtype)
        start += width
    for rider in riders:
        for out in (chip, section, both):
            out[:, start:] = rider[...]


def hop_sum_kernel(next_part, last_part, hop0, hop1, forth, back):
    cut = hop0.shape[0]

    def added(a, b):
        return (a.astype(F32) + b.astype(F32)).astype(BF16)

    forth[:cut] = added(next_part[:cut], hop0[...])
    forth[cut:] = next_part[cut:]
    back[:cut] = last_part[:cut]
    back[cut:] = added(last_part[cut:], hop1[...])


def whole_sum(own, parts):
    width = own.shape[1]
    total = own[...]
    for part in parts:
        total = total + part[:, :width].astype(F32)
    return total


def put_riders(four, rider, parts):
    width = rider.shape[1]
    four[0, 0] = rider[...]
    for k, part in enumerate(parts):
        four[(k + 1) // 2, (k + 1) % 2] = part[:, part.shape[1] - width :]


def put_units(features, hidden, unit_grads, packed):
    units = unit_grads.shape[1]
    unit_sums, square_sums = hidden[:, :units], hidden[:, units : units + 1]
    inverse_rms, hidden_pre, sigma, activated = row_terms(unit_sums, square_sums, features)
    scaled_grad, factor = unit_terms(
        unit_grads, unit_sums, inverse_rms, hidden_pre, sigma, features
    )
    packed[:, :units] = scaled_grad
    packed[:, units:] = jnp.broadcast_to(factor, (factor.shape[0], PAD)).astype(BF16)
    return activated


def first_unit_kernel(features, own, chip, section, both, packed, activated):
    units = activated.shape[1]
    total = whole_sum(own, (chip, section, both))
    activated[...] = put_units(features, total, total[:, units + PAD :], packed)


def active_kernel(features, own, chip, section, both, rider, hidden, activated, four):
    parts = (chip, section, both)
    total = whole_sum(own, parts)
    hidden[...] = total
    units = activated.shape[1]
    terms = row_terms(total[:, :units], total[:, units : units + 1], features)
    activated[...] = terms[3]
    put_riders(four, rider, parts)


def unit_kernel(features, hidden, own, chip, section, both, rider, packed, four):
    parts = (chip, section, both)
    put_units(features, hidden, whole_sum(own, parts), packed)
    put_riders(four, rider, parts)


def call(kernel, name, outs, args, scratch=(), specs=None, place=None, flops=0, out_spec=None):
    size = sum(a.size * a.dtype.itemsize for a in args)
    size += sum(o.size * o.dtype.itemsize for o in outs)
    cost = pl.CostEstimate(flops=flops, bytes_accessed=size, transcendentals=0)
    params = pltpu.CompilerParams(vmem_limit_bytes=VMEM_BYTES)
    if place is None:
        return pl.pallas_call(
            kernel, out_shape=outs, compiler_params=params, cost_estimate=cost, name=name
        )(*args)

    def whole(shape):
        return pl.BlockSpec(shape, lambda i, s: (0,) * len(shape))

    specs = specs or {}
    return pl.pallas_call(
        kernel,
        out_shape=outs,
        grid_spec=pltpu.PrefetchScalarGridSpec(
            num_scalar_prefetch=1,
            grid=(STEPS,),
            in_specs=[specs.get(k, whole(a.shape)) for k, a in enumerate(args)],
            out_specs=[out_spec or whole(o.shape) for o in outs],
            scratch_shapes=[pltpu.VMEM(shape, dtype) for shape, dtype in scratch],
        ),
        compiler_params=params,
        cost_estimate=cost,
        name=name,
    )(place, *args)


def shape_of(shape, dtype=BF16):
    return jax.ShapeDtypeStruct(shape, dtype)


def swap_chips(chip, section, both):
    return swap_chip(chip), swap_section(section), swap_both(both)


def core_sum(sent, kept, *riders):
    tokens = sent[0].shape[2]
    width = sum(part.shape[3] for part in sent)
    wide = width + sum(rider.shape[1] for rider in riders)

    def bound(*refs):
        core_sum_kernel(len(sent), *refs)

    return call(
        bound,
        "core_sum",
        [shape_of((tokens, width), F32)] + [shape_of((tokens, wide))] * 3,
        tuple(kept) + tuple(swap_core(part) for part in sent) + riders,
    )


def pair_spread(block, *earlier):
    parts = (block,) + swap_chips(block, block, block)
    four = after(jnp.stack(parts).reshape((2, 2) + block.shape), *earlier)
    return four, swap_core(four)


def two_sections(saved_inputs, cotangent, weight_in, weight_out, gain, plan):
    own = lax.axis_index("section")
    other = 1 - own
    mp_index = lax.axis_index("mp")
    stored = saved_inputs[0]
    slots, tokens, width = stored.shape
    half, part = slots // 2, width // 2
    features = width * lax.axis_size("mp")
    place = jnp.concatenate(
        (jnp.stack((mp_index % 2, mp_index // 2, own, other, own)).astype(jnp.int32), plan)
    )

    def rows(array, section):
        return lax.dynamic_slice_in_dim(array, section * part, part, 0)

    mine = (rows(weight_in[0], own), rows(weight_out[0], own))
    moved_in = swap_section(rows(weight_in[0], other))
    moved_out = swap_section(rows(weight_out[0], other))
    moved = (moved_in, moved_out)

    def sent_inputs(phase):
        first = half * place[OWN + phase]
        return lax.dynamic_slice(stored, (first, 0, other * part), (half, tokens, part))


    def near(block):
        return rotate(block, 1), rotate(block, -1)

    held0 = [jnp.where(own == 1, a, b) for a, b in zip(mine, moved)]
    held1 = jnp.where(own == 0, jnp.stack(mine), jnp.stack(moved))
    below_in, above_in = near(held0[0])
    below_out, above_out = near(held0[1])
    far_in, far_out = rotate(below_in, 1), rotate(above_out, -1)
    weights0 = (held0[0], above_in, far_in, below_in, held0[1], above_out, far_out, below_out)
    received = [swap_section(after(sent_inputs(0), moved_out)), None]
    received[1] = swap_section(after(sent_inputs(1), below_out))
    below, above = near(after(held1, below_out, above_out))
    weights1 = (held1, above, below, rotate(below[0], 1), rotate(above[1], -1))
    units = 4 * mine[0].shape[-1]
    rows2 = 2 * tokens
    gain_spec = pl.BlockSpec((2, part), lambda i, s: (0, s[SECTION]))
    top_spec = pl.BlockSpec((slots, tokens, part), lambda i, s: (0, 0, s[SECTION]))
    partial_shapes = [shape_of((2, 2, tokens, units))] * 2
    hidden_shapes = [shape_of((2, 2, tokens, units + PAD))] * 2
    set_shape = shape_of((half, tokens, part))
    weight_scratch = ((part, units), BF16)
    rows_scratch = ((rows2, part), BF16)
    spread_scratch = ((2, 2, 2, tokens, units + PAD), BF16)
    grad_shapes = [shape_of((units // 4, part), F32)] + [shape_of((units // 4, part))] * 3
    four_shape = shape_of((2, 2, tokens, units))
    one_dot = 2 * slots * tokens * part * units


    tile = part // STEPS
    tile_top = pl.BlockSpec((slots, tokens, tile), lambda i, s: (0, 0, STEPS * s[SECTION] + i))
    tile_gain = pl.BlockSpec((2, tile), lambda i, s: (0, STEPS * s[SECTION] + i))
    tile_set = pl.BlockSpec((half, tokens, tile), lambda i, s: (0, 0, i))
    tile_grad = pl.BlockSpec((units // 4, tile), lambda i, s: (0, i))
    grad_scratch = [((units, slots * tokens), BF16), ((slots * tokens, tile), BF16)]

    def tile_own(phase):
        return pl.BlockSpec(
            (half, tokens, tile), lambda i, s: (s[OWN + phase], 0, STEPS * s[SECTION] + i)
        )

    def own_spec(phase):
        return pl.BlockSpec(
            (half, tokens, part), lambda i, s: (s[OWN + phase], 0, s[SECTION])
        )

    def bind(kernel, *first):
        def bound(*refs):
            kernel(*first, *refs)

        return bound

    def first_hop(parts):
        cut = parts[2].shape[0] // 2
        return rotate(parts[2][:cut], 1), rotate(parts[2][cut:], -1)

    def second_hop(parts, hop, *earlier):
        kept, next_part, _, last_part = parts
        forth, back = call(
            hop_sum_kernel,
            "hop_sum",
            [shape_of(next_part.shape)] * 2,
            (after(next_part, *earlier), last_part) + hop,
        )
        return kept, rotate(forth, 1), rotate(back, -1)

    def total(parts):
        return parts[0] + parts[1].astype(F32) + parts[2].astype(F32)

    sent, kept, sent1, kept1 = call(
        bind(first_part_kernel, 1),
        "first_part",
        hidden_shapes + partial_shapes,
        (stored, received[0], gain, cotangent) + weights0,
        [weight_scratch, weight_scratch, rows_scratch],
        {0: own_spec(0), 2: gain_spec, 3: top_spec},
        place,
        2 * one_dot,
    )
    own_sum, *parts = core_sum((sent, sent1), (after(kept, received[1]), kept1))
    scaled0, act0 = call(
        bind(first_unit_kernel, features),
        "first_units",
        [shape_of((tokens, units + PAD)), shape_of((tokens, units))],
        (own_sum,) + swap_chips(*parts),
    )
    scaled0 = pair_spread(scaled0)

    sent, kept = call(
        bind(hidden_kernel, 0),
        "hidden_part",
        hidden_shapes,
        (stored, received[1], gain) + weights1,
        [weight_scratch, rows_scratch],
        {0: own_spec(1), 2: gain_spec},
        place,
        one_dot,
    )
    own_sum, *parts = core_sum((sent,), (kept,), act0)
    in_grads0 = call(
        bind(in_grad_kernel, 1),
        "in_grad",
        grad_shapes,
        (stored, received[0], after(gain, own_sum)) + scaled0,
        grad_scratch,
        {0: tile_own(0), 1: tile_set, 2: tile_gain},
        place,
        one_dot,
        tile_grad,
    )
    in_hop0 = first_hop(in_grads0)
    result0, result1, sent, kept = call(
        bind(first_back_kernel, 1),
        "first_back",
        [set_shape, set_shape] + partial_shapes,
        (stored, received[0], after(gain, in_grads0[0]), cotangent) + scaled0 + weights0[:4] + weights1,
        [weight_scratch, weight_scratch, spread_scratch, rows_scratch, rows_scratch],
        {0: own_spec(0), 2: gain_spec, 3: top_spec},
        place,
        2 * one_dot,
    )
    hidden1, act1, act0 = call(
        bind(active_kernel, features),
        "activated",
        [shape_of((tokens, units + PAD), F32), shape_of((tokens, units)), four_shape],
        (after(own_sum, kept),) + swap_chips(*parts) + (act0,),
    )
    own_sum, *parts = core_sum((after(sent, *in_hop0),), (kept,), act1)
    in_totals0 = second_hop(in_grads0, in_hop0, own_sum)
    out_grads0 = call(
        top_grad_kernel,
        "top_grad",
        grad_shapes,
        (cotangent, after(act0, own_sum), swap_core(act0)),
        grad_scratch,
        {0: tile_top},
        place,
        one_dot,
        tile_grad,
    )
    out_hop0 = first_hop(out_grads0)
    scaled1, act1 = call(
        bind(unit_kernel, features),
        "unit_grads",
        [shape_of((tokens, units + PAD)), four_shape],
        (after(hidden1, out_grads0[0], *in_totals0[1:]), own_sum) + swap_chips(*parts) + (act1,),
    )
    out_totals0 = second_hop(out_grads0, out_hop0, scaled1)
    scaled1 = pair_spread(scaled1, *out_hop0)
    out_grads1 = call(
        out_grad_kernel,
        "out_grad",
        grad_shapes,
        (result1, result0, act1, swap_core(act1)),
        grad_scratch,
        {0: tile_set, 1: tile_set},
        place,
        one_dot,
        tile_grad,
    )
    out_hop1 = first_hop(out_grads1)
    returned0 = swap_section(after(result1, scaled1[0]))
    result2, result3 = call(
        bind(last_back_kernel, 0),
        "last_back",
        [set_shape, set_shape],
        (stored, received[1], gain, result1, result0) + scaled1 + weights1,
        [weight_scratch, spread_scratch, rows_scratch, rows_scratch],
        {0: own_spec(1), 2: gain_spec},
        place,
        one_dot,
    )
    returned1 = swap_section(result3)
    in_grads1 = call(
        bind(in_grad_kernel, 0),
        "in_grad",
        grad_shapes,
        (stored, received[1], after(gain, out_grads1[0], result3)) + scaled1,
        grad_scratch,
        {0: tile_own(1), 1: tile_set, 2: tile_gain},
        place,
        one_dot,
        tile_grad,
    )
    in_hop1 = first_hop(in_grads1)
    in_totals1 = second_hop(in_grads1, in_hop1, returned0)
    out_totals1 = second_hop(out_grads1, out_hop1, in_grads1[0])
    in_total0, out_total0, out_total1 = total(in_totals0), total(out_totals0), total(out_totals1)
    in_total1 = total(in_totals1)
    outputs = jnp.zeros_like(stored)
    for phase, block, back in ((0, result0, returned0), (1, result2, returned1)):
        first = half * place[OWN + phase]
        outputs = lax.dynamic_update_slice(outputs, block, (first, 0, own * part))
        outputs = lax.dynamic_update_slice(outputs, back, (first, 0, other * part))

    def whole(total0, total1):
        kept = jnp.where(own == 1, total0, total1)
        given = jnp.where(own == 1, total1, total0).astype(BF16)
        back = after(swap_section(given), returned1).astype(F32)
        return jnp.where(
            own == 1,
            jnp.concatenate((back, kept), 1),
            jnp.concatenate((kept, back), 1),
        ).T

    return (whole(in_total0, in_total1)[None], whole(out_total0, out_total1)[None], outputs[None])


def pick(array, index, axis):
    return lax.dynamic_index_in_dim(array, index, axis, keepdims=False)


def any_sum(partial):
    sets, slots, tokens, width = partial.shape
    count = lax.axis_size("section") * lax.axis_size("mp")
    rows = partial.astype(BF16).reshape(count, sets * slots * tokens // count, width)
    moved = lax.all_to_all(rows, ("section", "mp"), 0, 0)
    return jnp.sum(moved.astype(F32), axis=0)


def any_spread(block, sets, slots, tokens):
    whole = lax.all_gather(block, ("section", "mp"), axis=0, tiled=True)
    return whole.reshape(sets, slots, tokens, block.shape[-1])


def row_terms(unit_sums, square_sums, features):
    inverse_rms = lax.rsqrt(square_sums / features + EPS)
    hidden_pre = inverse_rms * unit_sums
    sigma = jax.nn.sigmoid(hidden_pre)
    activated = (hidden_pre * sigma).astype(BF16)
    return inverse_rms, hidden_pre, sigma, activated


def unit_terms(unit_grads, unit_sums, inverse_rms, hidden_pre, sigma, features):
    grad_hidden = unit_grads * sigma * (1.0 + hidden_pre * (1.0 - sigma))
    scaled_grad = (inverse_rms * grad_hidden).astype(BF16)
    rms_term = jnp.sum(grad_hidden * unit_sums, axis=-1, keepdims=True)
    factor = inverse_rms**3 / features * rms_term
    return scaled_grad, factor


def project(rows, weights):
    return jnp.einsum("jktd,de->jkte", rows, weights, preferred_element_type=F32)


def accumulate(rows, units):
    return jnp.einsum("jktd,jkte->de", rows, units, preferred_element_type=F32)


def run_phase(stored, incoming, in_full, out_full, gain_row, features, sum_units, spread_units):
    units = in_full.shape[-1]
    wide = stored.astype(F32)
    normed = (wide * gain_row).astype(BF16)
    squares = jnp.sum(wide * wide, axis=-1, keepdims=True)
    part = project(normed, in_full)
    packed = jnp.concatenate((part, jnp.broadcast_to(squares, part.shape[:-1] + (PAD,))), axis=-1)
    hidden = sum_units(packed)
    unit_sums, square_sums = hidden[:, :units], hidden[:, units : units + 1]
    inverse_rms, hidden_pre, sigma, activated = row_terms(unit_sums, square_sums, features)
    activated = spread_units(activated)
    unit_grads = sum_units(project(incoming, out_full))
    scaled_grad, factor = unit_terms(
        unit_grads, unit_sums, inverse_rms, hidden_pre, sigma, features
    )
    factor = jnp.broadcast_to(factor.astype(BF16), (factor.shape[0], PAD))
    spread = spread_units(jnp.concatenate((scaled_grad, factor), axis=-1))
    scaled_grad, factor = spread[..., :units], spread[..., units : units + 1].astype(F32)
    back = jnp.einsum("jkte,de->jktd", scaled_grad, in_full, preferred_element_type=F32)
    result = (incoming.astype(F32) + gain_row * back - factor * wide).astype(BF16)
    return result, accumulate(normed, scaled_grad), accumulate(incoming, activated)


def any_sections(saved_inputs, cotangent, weight_in, weight_out, gain, plan):
    count = lax.axis_size("section")
    own = lax.axis_index("section")
    stored = saved_inputs[0]
    slots, tokens, width = stored.shape
    half, part = slots // 2, width // count
    features = width * lax.axis_size("mp")
    units = weight_in.shape[-1]

    def split_columns(array):
        return jnp.moveaxis(array.reshape(array.shape[:-1] + (count, part)), -2, 0)

    def moved(array):
        return lax.all_to_all(array, "section", 0, 0)

    inputs = moved(split_columns(stored))
    ins = moved(weight_in[0].reshape(count, part, units))
    outs = moved(weight_out[0].reshape(count, part, units))
    gains = pick(split_columns(gain), own, 0)
    top = lax.dynamic_slice_in_dim(cotangent, own * part, part, 2)
    incoming = jnp.stack([pick(top, plan[i], 0) for i in range(slots)])
    incoming = incoming.reshape(2, half, tokens, part)
    results = [[None, None] for _ in range(count)]
    in_blocks = [None] * count
    out_blocks = [None] * count
    for phase in range(count):
        group = count - 1 - phase
        result, in_total, out_total = run_phase(
            jnp.stack((inputs[group, :half], inputs[phase, half:])),
            incoming,
            gather_units(ins[group]),
            gather_units(outs[group]),
            gains[group],
            features,
            any_sum,
            lambda block: any_spread(block, 2, half, tokens),
        )
        in_blocks[group] = scatter_units(in_total)
        out_blocks[group] = scatter_units(out_total)
        results[group][0] = result[0]
        results[phase][1] = result[1]
        incoming = result

    def whole(blocks):
        return moved(jnp.stack(blocks).astype(BF16)).astype(F32).reshape(width, units)

    outputs = moved(jnp.stack([jnp.concatenate(pair) for pair in results]))
    outputs = jnp.moveaxis(outputs, 0, -2).reshape(stored.shape)
    return (whole(in_blocks)[None], whole(out_blocks)[None], outputs[None])


def solution(mesh):
    in_specs = (
        P("section", None, "dp", "mp"),
        P(None, "dp", "mp"),
        P("section", "mp", "dp"),
        P("section", "mp", "dp"),
        P(None, "mp"),
        P(),
    )
    out_specs = (P("section", "mp", "dp"), P("section", "mp", "dp"), P("section", None, "dp", "mp"))
    paired = mesh.shape["section"] == 2 and mesh.shape["mp"] == 4
    return jax.shard_map(
        two_sections if paired else any_sections,
        mesh=mesh,
        in_specs=in_specs,
        out_specs=out_specs,
        check_vma=False,
    )
```

```python
import jax
import jax.numpy as jnp
from jax import lax
from jax.experimental import pallas as pl
from jax.experimental.pallas import tpu as pltpu
from jax.sharding import PartitionSpec as P

EPS = 1e-05
F32 = jnp.float32
BF16 = jnp.bfloat16
PAD = 128


def rotate(block, shift):
    count = lax.axis_size("dp")
    return lax.ppermute(block, "dp", [(i, (i + shift) % count) for i in range(count)])


def gather_units(block):
    count = lax.axis_size("dp")
    return jnp.concatenate([block] + [rotate(block, -k) for k in range(1, count)], axis=-1)


def scatter_units(total):
    count = lax.axis_size("dp")
    width = total.shape[-1] // count
    parts = total.astype(BF16)
    kept = total[..., :width].astype(F32)
    for k in range(1, count):
        kept = kept + rotate(parts[..., k * width : (k + 1) * width], k).astype(F32)
    return kept


def swap_section(block):
    return lax.ppermute(block, "section", [(0, 1), (1, 0)])


def swap_core(block):
    return lax.ppermute(block, "mp", [(i, i ^ 1) for i in range(4)])


def swap_chip(block):
    return lax.ppermute(block, "mp", [(i, i ^ 2) for i in range(4)])


def swap_both(block):
    return lax.ppermute(block, ("section", "mp"), [(i, i ^ 6) for i in range(8)])


def after(array, *others):
    return lax.optimization_barrier((array,) + others)[0]


CORE, CHIP, SECTION, OWN, PLAN = 0, 1, 2, 3, 5
STEPS = 4
VMEM_BYTES = 44 * 1024 * 1024


def step_place():
    step = pl.program_id(0)
    return step, 1 - step // 2, step % 2


def slot_at(place, a, b):
    return 2 * (place[CHIP] ^ a) + (place[CORE] ^ b)


def join_units(step, which, parts, whole):
    held, above, below, *far = parts

    @pl.when(step == 0)
    def _():
        width = held.shape[-1]
        for k, part in enumerate((held.at[which], above.at[which], far[which], below.at[which])):
            whole[:, k * width : (k + 1) * width] = part[...]


def join_whole(step, parts, whole):
    @pl.when(step == 0)
    def _():
        for k, part in enumerate(parts):
            whole[:, k * part.shape[1] : (k + 1) * part.shape[1]] = part[...]


def join_slots(step, parts, whole):
    @pl.when(step == 0)
    def _():
        whole[0] = parts[0][...]
        whole[1] = parts[1][...]


def load_set(place, refs, rows):
    step, b, which = step_place()
    tokens = refs[0].shape[1]
    for k in range(2):

        @pl.when(which == k)
        def _(k=k):
            for a in range(2):
                rows[a * tokens : (a + 1) * tokens] = refs[k][slot_at(place, a, b)]


def load_top(phase, place, top, rows):
    step, b, which = step_place()
    tokens, half = top.shape[1], top.shape[0] // 2
    for a in range(2):
        slot = half * (place[OWN + phase] ^ which) + slot_at(place, a, b)
        rows[a * tokens : (a + 1) * tokens] = top[place[PLAN + slot]]


def put_partial(value, sent, kept, step, which):
    value = value.astype(BF16).reshape(sent.shape[1:])

    @pl.when(step < 2)
    def _():
        sent[which] = value

    @pl.when(step >= 2)
    def _():
        kept[which] = value


def hidden_kernel(group, place, own, received, gain, w0, w1, w2, w3, w4, sent, kept, weights, rows):
    step, b, which = step_place()
    join_units(step, 0, (w0, w1, w2, w3, w4), weights)
    load_set(place, (own, received), rows)
    wide = rows[...].astype(F32)
    normed = (wide * gain[group : group + 1, :]).astype(BF16)
    part = jnp.dot(normed, weights[...], preferred_element_type=F32)
    squares = jnp.sum(wide * wide, axis=1, keepdims=True)
    packed = jnp.concatenate((part, jnp.broadcast_to(squares, (part.shape[0], PAD))), axis=1)
    put_partial(packed, sent, kept, step, which)


def first_part_kernel(
    group, place, own, received, gain, top, w0, w1, w2, w3, w4, w5, w6, w7, sent0, kept0, sent1, kept1,
    weights, outward, rows,
):
    step, b, which = step_place()
    join_whole(step, (w0, w1, w2, w3), weights)
    join_whole(step, (w4, w5, w6, w7), outward)
    load_set(place, (own, received), rows)
    wide = rows[...].astype(F32)
    normed = (wide * gain[group : group + 1, :]).astype(BF16)
    part = jnp.dot(normed, weights[...], preferred_element_type=F32)
    squares = jnp.sum(wide * wide, axis=1, keepdims=True)
    packed = jnp.concatenate((part, jnp.broadcast_to(squares, (part.shape[0], PAD))), axis=1)
    put_partial(packed, sent0, kept0, step, which)
    load_top(0, place, top, rows)
    part = jnp.dot(rows[...], outward[...], preferred_element_type=F32)
    put_partial(part, sent1, kept1, step, which)


def back_step(group, place, own, received, gain, spread, weights, rows, incoming):
    step, b, which = step_place()
    load_set(place, (own, received), rows)
    units = weights.shape[1]
    packed = spread[b, which].reshape(rows.shape[0], units + PAD)
    back = lax.dot_general(
        packed[:, :units], weights[...], (((1,), (1,)), ((), ())), preferred_element_type=F32
    )
    factor = packed[:, units : units + 1].astype(F32)
    result = (
        incoming.astype(F32)
        + gain[group : group + 1, :] * back
        - factor * rows[...].astype(F32)
    )
    return result.astype(BF16)


def put_result(place, result, results):
    step, b, which = step_place()
    tokens = result.shape[0] // 2
    for k in range(2):

        @pl.when(which == k)
        def _(k=k):
            for a in range(2):
                results[k][slot_at(place, a, b)] = result[a * tokens : (a + 1) * tokens]


def first_back_kernel(
    group, place, own, received, gain, top, p0, p1, w0, w1, w2, w3, v0, v1, v2, v3, v4,
    result0, result1, sent, kept, weights, outward, spread, rows, grads,
):
    step, b, which = step_place()
    join_whole(step, (w0, w1, w2, w3), weights)
    join_units(step, 1, (v0, v1, v2, v3, v4), outward)
    join_slots(step, (p0, p1), spread)
    load_top(0, place, top, grads)
    result = back_step(group, place, own, received, gain, spread, weights, rows, grads[...])
    put_result(place, result, (result0, result1))
    part = jnp.dot(result, outward[...], preferred_element_type=F32)
    put_partial(part, sent, kept, step, 1 - which)


def last_back_kernel(
    group, place, own, received, gain, in0, in1, p0, p1, w0, w1, w2, w3, w4,
    result0, result1, weights, spread, rows, grads,
):
    step, b, which = step_place()
    join_units(step, 0, (w0, w1, w2, w3, w4), weights)
    join_slots(step, (p0, p1), spread)
    load_set(place, (in0, in1), grads)
    result = back_step(group, place, own, received, gain, spread, weights, rows, grads[...])
    put_result(place, result, (result0, result1))


def flip_slots(parts, flipped):
    @pl.when(pl.program_id(0) == 0)
    def _():
        units = flipped.shape[0]
        for k in range(8):
            block = parts[k // 4][k // 2 % 2, k % 2]
            tokens = block.shape[0]
            flipped[:, k * tokens : (k + 1) * tokens] = block[:, :units].T


def fill_rows(place, load, rows):
    for k in range(8):
        block = load(k // 2 % 2, slot_at(place, k % 2, k // 4))
        tokens = block.shape[0]
        rows[k * tokens : (k + 1) * tokens] = block


def put_grad(flipped, rows, kept, parts):
    value = jnp.dot(flipped[...], rows[...], preferred_element_type=F32)
    height = kept.shape[0]
    kept[...] = value[:height]
    for k, part in enumerate(parts):
        part[...] = value[(k + 1) * height : (k + 2) * height].astype(BF16)


def in_grad_kernel(
    group, place, own, received, gain, p0, p1, kept, c1, c2, c3, flipped, rows
):
    def load(which, slot):
        block = (own, received)[which][slot].astype(F32)
        return (block * gain[group : group + 1, :]).astype(BF16)

    flip_slots((p0, p1), flipped)
    fill_rows(place, load, rows)
    put_grad(flipped, rows, kept, (c1, c2, c3))


def top_grad_kernel(place, top, p0, p1, kept, c1, c2, c3, flipped, rows):
    half = top.shape[0] // 2

    def load(which, slot):
        return top[place[PLAN + half * (place[OWN] ^ which) + slot]]

    flip_slots((p0, p1), flipped)
    fill_rows(place, load, rows)
    put_grad(flipped, rows, kept, (c1, c2, c3))


def out_grad_kernel(place, in0, in1, p0, p1, kept, c1, c2, c3, flipped, rows):
    flip_slots((p0, p1), flipped)
    fill_rows(place, lambda which, slot: (in0, in1)[which][slot], rows)
    put_grad(flipped, rows, kept, (c1, c2, c3))


def core_sum_kernel(count, *refs):
    kept, moved, riders = refs[:count], refs[count : 2 * count], refs[2 * count : -4]
    own, chip, section, both = refs[-4:]
    start = 0
    for left, right in zip(kept, moved):
        width = left.shape[-1]
        for k, out in enumerate((own, chip, section, both)):
            value = left[k // 2, k % 2].astype(F32) + right[k // 2, k % 2].astype(F32)
            out[:, start : start + width] = value.astype(out.dtype)
        start += width
    for rider in riders:
        for out in (chip, section, both):
            out[:, start:] = rider[...]


def hop_sum_kernel(next_part, last_part, hop0, hop1, forth, back):
    cut = hop0.shape[0]

    def added(a, b):
        return (a.astype(F32) + b.astype(F32)).astype(BF16)

    forth[:cut] = added(next_part[:cut], hop0[...])
    forth[cut:] = next_part[cut:]
    back[:cut] = last_part[:cut]
    back[cut:] = added(last_part[cut:], hop1[...])


def whole_sum(own, parts):
    width = own.shape[1]
    total = own[...]
    for part in parts:
        total = total + part[:, :width].astype(F32)
    return total


def put_riders(four, rider, parts):
    width = rider.shape[1]
    four[0, 0] = rider[...]
    for k, part in enumerate(parts):
        four[(k + 1) // 2, (k + 1) % 2] = part[:, part.shape[1] - width :]


def put_units(features, hidden, unit_grads, packed):
    units = unit_grads.shape[1]
    unit_sums, square_sums = hidden[:, :units], hidden[:, units : units + 1]
    inverse_rms, hidden_pre, sigma, activated = row_terms(unit_sums, square_sums, features)
    scaled_grad, factor = unit_terms(
        unit_grads, unit_sums, inverse_rms, hidden_pre, sigma, features
    )
    packed[:, :units] = scaled_grad
    packed[:, units:] = jnp.broadcast_to(factor, (factor.shape[0], PAD)).astype(BF16)
    return activated


def first_unit_kernel(features, own, chip, section, both, packed, activated):
    units = activated.shape[1]
    total = whole_sum(own, (chip, section, both))
    activated[...] = put_units(features, total, total[:, units + PAD :], packed)


def active_kernel(features, own, chip, section, both, rider, hidden, activated, four):
    parts = (chip, section, both)
    total = whole_sum(own, parts)
    hidden[...] = total
    units = activated.shape[1]
    terms = row_terms(total[:, :units], total[:, units : units + 1], features)
    activated[...] = terms[3]
    put_riders(four, rider, parts)


def unit_kernel(features, hidden, own, chip, section, both, rider, packed, four):
    parts = (chip, section, both)
    put_units(features, hidden, whole_sum(own, parts), packed)
    put_riders(four, rider, parts)


def call(kernel, name, outs, args, scratch=(), specs=None, place=None, flops=0, out_spec=None):
    size = sum(a.size * a.dtype.itemsize for a in args)
    size += sum(o.size * o.dtype.itemsize for o in outs)
    cost = pl.CostEstimate(flops=flops, bytes_accessed=size, transcendentals=0)
    params = pltpu.CompilerParams(vmem_limit_bytes=VMEM_BYTES)
    if place is None:
        return pl.pallas_call(
            kernel, out_shape=outs, compiler_params=params, cost_estimate=cost, name=name
        )(*args)

    def whole(shape):
        return pl.BlockSpec(shape, lambda i, s: (0,) * len(shape))

    specs = specs or {}
    return pl.pallas_call(
        kernel,
        out_shape=outs,
        grid_spec=pltpu.PrefetchScalarGridSpec(
            num_scalar_prefetch=1,
            grid=(STEPS,),
            in_specs=[specs.get(k, whole(a.shape)) for k, a in enumerate(args)],
            out_specs=[out_spec or whole(o.shape) for o in outs],
            scratch_shapes=[pltpu.VMEM(shape, dtype) for shape, dtype in scratch],
        ),
        compiler_params=params,
        cost_estimate=cost,
        name=name,
    )(place, *args)


def shape_of(shape, dtype=BF16):
    return jax.ShapeDtypeStruct(shape, dtype)


def swap_chips(chip, section, both):
    return swap_chip(chip), swap_section(section), swap_both(both)


def core_sum(sent, kept, *riders):
    tokens = sent[0].shape[2]
    width = sum(part.shape[3] for part in sent)
    wide = width + sum(rider.shape[1] for rider in riders)

    def bound(*refs):
        core_sum_kernel(len(sent), *refs)

    return call(
        bound,
        "core_sum",
        [shape_of((tokens, width), F32)] + [shape_of((tokens, wide))] * 3,
        tuple(kept) + tuple(swap_core(part) for part in sent) + riders,
    )


def pair_spread(block, *earlier):
    parts = (block,) + swap_chips(block, block, block)
    four = after(jnp.stack(parts).reshape((2, 2) + block.shape), *earlier)
    return four, swap_core(four)


def two_sections(saved_inputs, cotangent, weight_in, weight_out, gain, plan):
    own = lax.axis_index("section")
    other = 1 - own
    mp_index = lax.axis_index("mp")
    stored = saved_inputs[0]
    slots, tokens, width = stored.shape
    half, part = slots // 2, width // 2
    features = width * lax.axis_size("mp")
    place = jnp.concatenate(
        (jnp.stack((mp_index % 2, mp_index // 2, own, other, own)).astype(jnp.int32), plan)
    )

    def rows(array, section):
        return lax.dynamic_slice_in_dim(array, section * part, part, 0)

    mine = (rows(weight_in[0], own), rows(weight_out[0], own))
    moved_in = swap_section(rows(weight_in[0], other))
    moved_out = swap_section(rows(weight_out[0], other))
    moved = (moved_in, moved_out)

    def sent_inputs(phase):
        first = half * place[OWN + phase]
        return lax.dynamic_slice(stored, (first, 0, other * part), (half, tokens, part))


    def near(block):
        return rotate(block, 1), rotate(block, -1)

    held0 = [jnp.where(own == 1, a, b) for a, b in zip(mine, moved)]
    held1 = jnp.where(own == 0, jnp.stack(mine), jnp.stack(moved))
    below_in, above_in = near(held0[0])
    below_out, above_out = near(held0[1])
    far_in, far_out = rotate(below_in, 1), rotate(above_out, -1)
    weights0 = (held0[0], above_in, far_in, below_in, held0[1], above_out, far_out, below_out)
    received = [swap_section(after(sent_inputs(0), moved_out)), None]
    received[1] = swap_section(after(sent_inputs(1), below_out))
    below, above = near(after(held1, below_out, above_out))
    weights1 = (held1, above, below, rotate(below[0], 1), rotate(above[1], -1))
    units = 4 * mine[0].shape[-1]
    rows2 = 2 * tokens
    gain_spec = pl.BlockSpec((2, part), lambda i, s: (0, s[SECTION]))
    top_spec = pl.BlockSpec((slots, tokens, part), lambda i, s: (0, 0, s[SECTION]))
    partial_shapes = [shape_of((2, 2, tokens, units))] * 2
    hidden_shapes = [shape_of((2, 2, tokens, units + PAD))] * 2
    set_shape = shape_of((half, tokens, part))
    weight_scratch = ((part, units), BF16)
    rows_scratch = ((rows2, part), BF16)
    spread_scratch = ((2, 2, 2, tokens, units + PAD), BF16)
    grad_shapes = [shape_of((units // 4, part), F32)] + [shape_of((units // 4, part))] * 3
    four_shape = shape_of((2, 2, tokens, units))
    one_dot = 2 * slots * tokens * part * units


    tile = part // STEPS
    tile_top = pl.BlockSpec((slots, tokens, tile), lambda i, s: (0, 0, STEPS * s[SECTION] + i))
    tile_gain = pl.BlockSpec((2, tile), lambda i, s: (0, STEPS * s[SECTION] + i))
    tile_set = pl.BlockSpec((half, tokens, tile), lambda i, s: (0, 0, i))
    tile_grad = pl.BlockSpec((units // 4, tile), lambda i, s: (0, i))
    grad_scratch = [((units, slots * tokens), BF16), ((slots * tokens, tile), BF16)]

    def tile_own(phase):
        return pl.BlockSpec(
            (half, tokens, tile), lambda i, s: (s[OWN + phase], 0, STEPS * s[SECTION] + i)
        )

    def own_spec(phase):
        return pl.BlockSpec(
            (half, tokens, part), lambda i, s: (s[OWN + phase], 0, s[SECTION])
        )

    def bind(kernel, *first):
        def bound(*refs):
            kernel(*first, *refs)

        return bound

    def first_hop(parts):
        cut = parts[2].shape[0] // 2
        return rotate(parts[2][:cut], 1), rotate(parts[2][cut:], -1)

    def second_hop(parts, hop, *earlier):
        kept, next_part, _, last_part = parts
        forth, back = call(
            hop_sum_kernel,
            "hop_sum",
            [shape_of(next_part.shape)] * 2,
            (after(next_part, *earlier), last_part) + hop,
        )
        return kept, rotate(forth, 1), rotate(back, -1)

    def total(parts):
        return parts[0] + parts[1].astype(F32) + parts[2].astype(F32)

    sent, kept, sent1, kept1 = call(
        bind(first_part_kernel, 1),
        "first_part",
        hidden_shapes + partial_shapes,
        (stored, received[0], gain, cotangent) + weights0,
        [weight_scratch, weight_scratch, rows_scratch],
        {0: own_spec(0), 2: gain_spec, 3: top_spec},
        place,
        2 * one_dot,
    )
    own_sum, *parts = core_sum((sent, sent1), (after(kept, received[1]), kept1))
    scaled0, act0 = call(
        bind(first_unit_kernel, features),
        "first_units",
        [shape_of((tokens, units + PAD)), shape_of((tokens, units))],
        (own_sum,) + swap_chips(*parts),
    )
    scaled0 = pair_spread(scaled0)

    sent, kept = call(
        bind(hidden_kernel, 0),
        "hidden_part",
        hidden_shapes,
        (stored, received[1], gain) + weights1,
        [weight_scratch, rows_scratch],
        {0: own_spec(1), 2: gain_spec},
        place,
        one_dot,
    )
    own_sum, *parts = core_sum((sent,), (kept,), act0)
    in_grads0 = call(
        bind(in_grad_kernel, 1),
        "in_grad",
        grad_shapes,
        (stored, received[0], after(gain, own_sum)) + scaled0,
        grad_scratch,
        {0: tile_own(0), 1: tile_set, 2: tile_gain},
        place,
        one_dot,
        tile_grad,
    )
    in_hop0 = first_hop(in_grads0)
    result0, result1, sent, kept = call(
        bind(first_back_kernel, 1),
        "first_back",
        [set_shape, set_shape] + partial_shapes,
        (stored, received[0], after(gain, in_grads0[0]), cotangent) + scaled0 + weights0[:4] + weights1,
        [weight_scratch, weight_scratch, spread_scratch, rows_scratch, rows_scratch],
        {0: own_spec(0), 2: gain_spec, 3: top_spec},
        place,
        2 * one_dot,
    )
    hidden1, act1, act0 = call(
        bind(active_kernel, features),
        "activated",
        [shape_of((tokens, units + PAD), F32), shape_of((tokens, units)), four_shape],
        (after(own_sum, kept),) + swap_chips(*parts) + (act0,),
    )
    own_sum, *parts = core_sum((after(sent, *in_hop0),), (kept,), act1)
    in_totals0 = second_hop(in_grads0, in_hop0, own_sum)
    out_grads0 = call(
        top_grad_kernel,
        "top_grad",
        grad_shapes,
        (cotangent, after(act0, own_sum), swap_core(act0)),
        grad_scratch,
        {0: tile_top},
        place,
        one_dot,
        tile_grad,
    )
    out_hop0 = first_hop(out_grads0)
    scaled1, act1 = call(
        bind(unit_kernel, features),
        "unit_grads",
        [shape_of((tokens, units + PAD)), four_shape],
        (after(hidden1, out_grads0[0], *in_totals0[1:]), own_sum) + swap_chips(*parts) + (act1,),
    )
    out_totals0 = second_hop(out_grads0, out_hop0, scaled1)
    scaled1 = pair_spread(scaled1, *out_hop0)
    out_grads1 = call(
        out_grad_kernel,
        "out_grad",
        grad_shapes,
        (result1, result0, act1, swap_core(act1)),
        grad_scratch,
        {0: tile_set, 1: tile_set},
        place,
        one_dot,
        tile_grad,
    )
    out_hop1 = first_hop(out_grads1)
    returned0 = swap_section(after(result1, scaled1[0]))
    result2, result3 = call(
        bind(last_back_kernel, 0),
        "last_back",
        [set_shape, set_shape],
        (stored, received[1], gain, result1, result0) + scaled1 + weights1,
        [weight_scratch, spread_scratch, rows_scratch, rows_scratch],
        {0: own_spec(1), 2: gain_spec},
        place,
        one_dot,
    )
    returned1 = swap_section(result3)
    in_grads1 = call(
        bind(in_grad_kernel, 0),
        "in_grad",
        grad_shapes,
        (stored, received[1], after(gain, out_grads1[0], result3)) + scaled1,
        grad_scratch,
        {0: tile_own(1), 1: tile_set, 2: tile_gain},
        place,
        one_dot,
        tile_grad,
    )
    in_hop1 = first_hop(after(in_grads1, *out_totals0[1:]))
    in_totals1 = second_hop(in_grads1, in_hop1, returned0)
    out_totals1 = second_hop(out_grads1, out_hop1, in_grads1[0])
    in_total0, out_total0, out_total1 = total(in_totals0), total(out_totals0), total(out_totals1)
    in_total1 = total(in_totals1)
    outputs = jnp.zeros_like(stored)
    for phase, block, back in ((0, result0, returned0), (1, result2, returned1)):
        first = half * place[OWN + phase]
        outputs = lax.dynamic_update_slice(outputs, block, (first, 0, own * part))
        outputs = lax.dynamic_update_slice(outputs, back, (first, 0, other * part))

    def whole(total0, total1):
        kept = jnp.where(own == 1, total0, total1)
        given = jnp.where(own == 1, total1, total0).astype(BF16)
        back = after(swap_section(given), returned1).astype(F32)
        return jnp.where(
            own == 1,
            jnp.concatenate((back, kept), 1),
            jnp.concatenate((kept, back), 1),
        ).T

    return (whole(in_total0, in_total1)[None], whole(out_total0, out_total1)[None], outputs[None])


def pick(array, index, axis):
    return lax.dynamic_index_in_dim(array, index, axis, keepdims=False)


def any_sum(partial):
    sets, slots, tokens, width = partial.shape
    count = lax.axis_size("section") * lax.axis_size("mp")
    rows = partial.astype(BF16).reshape(count, sets * slots * tokens // count, width)
    moved = lax.all_to_all(rows, ("section", "mp"), 0, 0)
    return jnp.sum(moved.astype(F32), axis=0)


def any_spread(block, sets, slots, tokens):
    whole = lax.all_gather(block, ("section", "mp"), axis=0, tiled=True)
    return whole.reshape(sets, slots, tokens, block.shape[-1])


def row_terms(unit_sums, square_sums, features):
    inverse_rms = lax.rsqrt(square_sums / features + EPS)
    hidden_pre = inverse_rms * unit_sums
    sigma = jax.nn.sigmoid(hidden_pre)
    activated = (hidden_pre * sigma).astype(BF16)
    return inverse_rms, hidden_pre, sigma, activated


def unit_terms(unit_grads, unit_sums, inverse_rms, hidden_pre, sigma, features):
    grad_hidden = unit_grads * sigma * (1.0 + hidden_pre * (1.0 - sigma))
    scaled_grad = (inverse_rms * grad_hidden).astype(BF16)
    rms_term = jnp.sum(grad_hidden * unit_sums, axis=-1, keepdims=True)
    factor = inverse_rms**3 / features * rms_term
    return scaled_grad, factor


def project(rows, weights):
    return jnp.einsum("jktd,de->jkte", rows, weights, preferred_element_type=F32)


def accumulate(rows, units):
    return jnp.einsum("jktd,jkte->de", rows, units, preferred_element_type=F32)


def run_phase(stored, incoming, in_full, out_full, gain_row, features, sum_units, spread_units):
    units = in_full.shape[-1]
    wide = stored.astype(F32)
    normed = (wide * gain_row).astype(BF16)
    squares = jnp.sum(wide * wide, axis=-1, keepdims=True)
    part = project(normed, in_full)
    packed = jnp.concatenate((part, jnp.broadcast_to(squares, part.shape[:-1] + (PAD,))), axis=-1)
    hidden = sum_units(packed)
    unit_sums, square_sums = hidden[:, :units], hidden[:, units : units + 1]
    inverse_rms, hidden_pre, sigma, activated = row_terms(unit_sums, square_sums, features)
    activated = spread_units(activated)
    unit_grads = sum_units(project(incoming, out_full))
    scaled_grad, factor = unit_terms(
        unit_grads, unit_sums, inverse_rms, hidden_pre, sigma, features
    )
    factor = jnp.broadcast_to(factor.astype(BF16), (factor.shape[0], PAD))
    spread = spread_units(jnp.concatenate((scaled_grad, factor), axis=-1))
    scaled_grad, factor = spread[..., :units], spread[..., units : units + 1].astype(F32)
    back = jnp.einsum("jkte,de->jktd", scaled_grad, in_full, preferred_element_type=F32)
    result = (incoming.astype(F32) + gain_row * back - factor * wide).astype(BF16)
    return result, accumulate(normed, scaled_grad), accumulate(incoming, activated)


def any_sections(saved_inputs, cotangent, weight_in, weight_out, gain, plan):
    count = lax.axis_size("section")
    own = lax.axis_index("section")
    stored = saved_inputs[0]
    slots, tokens, width = stored.shape
    half, part = slots // 2, width // count
    features = width * lax.axis_size("mp")
    units = weight_in.shape[-1]

    def split_columns(array):
        return jnp.moveaxis(array.reshape(array.shape[:-1] + (count, part)), -2, 0)

    def moved(array):
        return lax.all_to_all(array, "section", 0, 0)

    inputs = moved(split_columns(stored))
    ins = moved(weight_in[0].reshape(count, part, units))
    outs = moved(weight_out[0].reshape(count, part, units))
    gains = pick(split_columns(gain), own, 0)
    top = lax.dynamic_slice_in_dim(cotangent, own * part, part, 2)
    incoming = jnp.stack([pick(top, plan[i], 0) for i in range(slots)])
    incoming = incoming.reshape(2, half, tokens, part)
    results = [[None, None] for _ in range(count)]
    in_blocks = [None] * count
    out_blocks = [None] * count
    for phase in range(count):
        group = count - 1 - phase
        result, in_total, out_total = run_phase(
            jnp.stack((inputs[group, :half], inputs[phase, half:])),
            incoming,
            gather_units(ins[group]),
            gather_units(outs[group]),
            gains[group],
            features,
            any_sum,
            lambda block: any_spread(block, 2, half, tokens),
        )
        in_blocks[group] = scatter_units(in_total)
        out_blocks[group] = scatter_units(out_total)
        results[group][0] = result[0]
        results[phase][1] = result[1]
        incoming = result

    def whole(blocks):
        return moved(jnp.stack(blocks).astype(BF16)).astype(F32).reshape(width, units)

    outputs = moved(jnp.stack([jnp.concatenate(pair) for pair in results]))
    outputs = jnp.moveaxis(outputs, 0, -2).reshape(stored.shape)
    return (whole(in_blocks)[None], whole(out_blocks)[None], outputs[None])


def solution(mesh):
    in_specs = (
        P("section", None, "dp", "mp"),
        P(None, "dp", "mp"),
        P("section", "mp", "dp"),
        P("section", "mp", "dp"),
        P(None, "mp"),
        P(),
    )
    out_specs = (P("section", "mp", "dp"), P("section", "mp", "dp"), P("section", None, "dp", "mp"))
    paired = mesh.shape["section"] == 2 and mesh.shape["mp"] == 4
    return jax.shard_map(
        two_sections if paired else any_sections,
        mesh=mesh,
        in_specs=in_specs,
        out_specs=out_specs,
        check_vma=False,
    )
```
